32 devices in a mesh: tile: 8 (over z, x), batch: 4 (over y, core).
Axes of the slice: x: 2, y: 2, z: 4, core: 2. Of those that a mesh axis runs over, the one named last changes fastest.
Arguments:
- object_slices: float32 [8, 2, 2, 256, 256], P('tile'), may hold values from -1 to 1
- probe: float32 [2, 2, 128, 128], replicated, may hold values from -6 to 6
- prop_phase: float32 [128, 128], replicated, may hold values from -3.140625 to 3.140625
- scan_offsets: int32 [8, 4, 2], P('tile', 'batch'), may hold values from 0 to 255, as said below
- measured: float32 [8, 4, 128, 128], P('tile', 'batch'), may hold values from 0 to 2
Outputs:
- object_grad: float32 [8, 2, 2, 256, 256], P('tile', None, None, 'batch')
- probe_step: float32 [2, 2, 128, 128], replicated
The draws below stay inside these ranges and needn't reach their ends.
Inputs may be any that keep to these rules, and one draw needn't show every extreme that they name: `scan_offsets`: offsets are relative to the tile that holds the position. A window never leaves the object: in the last row of the tile grid the row offset is at most 128, in the last column of the tile grid the column offset is at most 128.
All inputs are finite; a program needn't handle non-finite values.
Results may differ from the reference program's by a relative error of at most 0.00012.
Values sent between devices are 32-bit elements; how exact they have to be, the bound alone decides.
No kernel may reach another device: no remote copies, remote signals or barrier semaphores. Data moves between devices by JAX's collectives and lax.ppermute only.
A program may use at most 64 MiB of HBM per device.

```python
import math
import jax
import jax.numpy as jnp
from jax import lax

W = 128
MODES = 2
NSL = 2
TS = 256
TGX = 8
TILES = 8
TGY = 1
SLOTS = 4
POSITIONS = 32


def draw_scan_offsets(key, part):
    tile_index = jnp.arange(TILES, dtype=jnp.int32)
    grid_rows = TILES // TGX
    row_limit = jnp.where(tile_index // TGX < grid_rows - 1, TS, TS - W + 1)
    col_limit = jnp.where(tile_index % TGX < TGX - 1, TS, TS - W + 1)
    limits = jnp.stack([row_limit, col_limit], axis=1)[:, None, :]
    values = jax.random.randint(key, (TILES, SLOTS, 2), 0, limits, dtype=jnp.int32)
    values = values.at[0, 0, 0].set(0).at[0, 0, 1].set(TS - 1)
    return values


def block_levels(own_key, shape, cuts, smallest, high):
    gain, own = 1.0, jax.random.fold_in(own_key, 6)
    for position, parts in cuts:
        draws = jnp.exp(jax.random.uniform(jax.random.fold_in(own, position), (parts,), jnp.float32, smallest / len(cuts), high / len(cuts)))
        gain = gain * jnp.repeat(draws, shape[position] // parts).reshape([-1 if axis == position else 1 for axis in range(len(shape))])
    return gain


def normal_values(own_key, dims, scale, bound, kind=jnp.bfloat16):
    drawn = scale * jax.random.normal(own_key, dims, jnp.float32)
    return jnp.clip(drawn, min=-bound, max=bound).astype(kind)


def setup_inputs(seed: int = 0) -> dict:
    seeds = jax.random.split(jax.random.key(seed), 6)
    object_slices = jnp.clip(jax.random.uniform(seeds[0], (TILES, NSL, 2, TS, TS), jnp.float32, -1.0, 1.0) * block_levels(seeds[0], (TILES, NSL, 2, TS, TS), ((0, 8),), -0.4, 0.0), -1.0, 1.0)
    probe = normal_values(seeds[1], (MODES, 2, W, W), 1.0, 6.0, jnp.float32)
    prop_phase = jnp.clip(jax.random.uniform(seeds[2], (W, W), jnp.float32, -3.140625, 3.140625), -3.140625, 3.140625)
    scan_offsets = draw_scan_offsets(jax.random.fold_in(seeds[5], 71), 0)
    measured = jnp.clip(2.0 * jax.random.uniform(seeds[4], (TILES, SLOTS, W, W), jnp.float32) ** block_levels(seeds[4], (TILES, SLOTS, W, W), ((0, 8), (1, 4)), -0.2, 0.2), 0.0, 2.0)
    return {"object_slices": object_slices, "probe": probe, "prop_phase": prop_phase, "scan_offsets": scan_offsets, "measured": measured}


LOSS_SCALE = 0.05

def fourier_tables(extent):
    indices = jnp.arange(extent, dtype=jnp.int32)
    phases = (indices[:, None] * indices[None, :] % extent).astype(jnp.float32) * (2.0 * math.pi / extent)
    scaling = 1.0 / math.sqrt(extent)
    return (jnp.cos(phases) * scaling, -jnp.sin(phases) * scaling)

def complex_product(left_op, right_op):
    return (left_op[0] * right_op[0] - left_op[1] * right_op[1], left_op[0] * right_op[1] + left_op[1] * right_op[0])

def transform(fields, table_real, table_imag):
    highest = lax.Precision.HIGHEST
    left_real = jnp.einsum('jk,bkl->bjl', table_real, fields[0], precision=highest) - jnp.einsum('jk,bkl->bjl', table_imag, fields[1], precision=highest)
    left_imag = jnp.einsum('jk,bkl->bjl', table_real, fields[1], precision=highest) + jnp.einsum('jk,bkl->bjl', table_imag, fields[0], precision=highest)
    out_real = jnp.einsum('bjk,kl->bjl', left_real, table_real, precision=highest) - jnp.einsum('bjk,kl->bjl', left_imag, table_imag, precision=highest)
    out_imag = jnp.einsum('bjk,kl->bjl', left_real, table_imag, precision=highest) + jnp.einsum('bjk,kl->bjl', left_imag, table_real, precision=highest)
    return (out_real, out_imag)

def window_loss(windows, probe, prop_real, prop_imag, target):
    positions = windows.shape[0]
    layers = windows.shape[1]
    mode_count = probe.shape[0]
    extent = probe.shape[-1]
    table_real, table_imag = fourier_tables(extent)
    shape_full = (positions, mode_count, extent, extent)
    shape_flat = (positions * mode_count, extent, extent)
    wavefield = (jnp.broadcast_to(probe[None, :, 0], shape_full), jnp.broadcast_to(probe[None, :, 1], shape_full))
    for slab_index in range(layers):
        if slab_index > 0:
            flattened = (wavefield[0].reshape(shape_flat), wavefield[1].reshape(shape_flat))
            spectrum = complex_product(transform(flattened, table_real, table_imag), (prop_real, prop_imag))
            flattened = transform(spectrum, table_real, -table_imag)
            wavefield = (flattened[0].reshape(shape_full), flattened[1].reshape(shape_full))
        slab_now = (windows[:, slab_index, 0][:, None], windows[:, slab_index, 1][:, None])
        wavefield = complex_product(wavefield, slab_now)
    far_field = transform((wavefield[0].reshape(shape_flat), wavefield[1].reshape(shape_flat)), table_real, table_imag)
    intensity = lax.optimization_barrier(jnp.sum((far_field[0] * far_field[0] + far_field[1] * far_field[1]).reshape(shape_full), axis=1))
    return LOSS_SCALE * jnp.sum((intensity - target) ** 2)

def reference(object_slices, probe, prop_phase, scan_offsets, measured):
    prop_real = jnp.cos(prop_phase)
    prop_imag = jnp.sin(prop_phase)
    frame = object_slices.reshape(TGY, TGX, NSL, 2, TS, TS).transpose(2, 3, 0, 4, 1, 5).reshape(NSL, 2, TGY * TS, TGX * TS)
    tile_index = jnp.arange(TILES, dtype=jnp.int32)
    row_anchor = (tile_index // TGX * TS)[:, None] + scan_offsets[:, :, 0]
    col_anchor = (tile_index % TGX * TS)[:, None] + scan_offsets[:, :, 1]
    zero_index = jnp.zeros((), jnp.int32)

    def cut_window(row_at, col_at):
        return lax.dynamic_slice(frame, (zero_index, zero_index, row_at, col_at), (NSL, 2, W, W))

    def per_tile(carry, inputs):
        grad_frame, probe_total = carry
        rows_here, cols_here, target = inputs
        windows = jax.vmap(cut_window)(rows_here, cols_here)
        window_grad, probe_grad = jax.grad(window_loss, argnums=(0, 1))(windows, probe, prop_real, prop_imag, target)

        def add_window(slot_index, frame_accum):
            start = (zero_index, zero_index, rows_here[slot_index], cols_here[slot_index])
            current = lax.dynamic_slice(frame_accum, start, (NSL, 2, W, W))
            return lax.dynamic_update_slice(frame_accum, current + window_grad[slot_index], start)
        grad_frame = lax.fori_loop(0, SLOTS, add_window, grad_frame)
        return ((grad_frame, probe_total + probe_grad), None)
    initial = (jnp.zeros(frame.shape, jnp.float32), jnp.zeros(probe.shape, jnp.float32))
    (grad_frame, probe_total), _ = lax.scan(per_tile, initial, (row_anchor, col_anchor, measured))
    object_grad = grad_frame.reshape(NSL, 2, TGY, TS, TGX, TS).transpose(2, 4, 0, 1, 3, 5).reshape(TILES, NSL, 2, TS, TS)
    return (object_grad, probe_total / POSITIONS)
```

```python
import functools
import math

import jax
import jax.numpy as jnp
import numpy as np
from jax import lax
from jax.experimental import pallas as pl
from jax.experimental.pallas import tpu as pltpu
from jax.sharding import PartitionSpec as P

TGX = 8


LOSS_SCALE = 0.05

F32 = jnp.float32
BF16 = jnp.bfloat16
ROWS = 8


def passed_along(block, axis, distance):
    devices = range(lax.axis_size(axis))
    route = [(i - distance, i) for i in devices if i - distance in devices]
    return lax.ppermute(block, axis, route)


def exchanged(block, axis, bit):
    return lax.ppermute(block, axis, [(i, i ^ bit) for i in range(lax.axis_size(axis))])


def fourier_tables(extent):
    indices = np.arange(extent)
    phases = (indices[:, None] * indices[None, :] % extent) * (2.0 * math.pi / extent)
    tables = np.stack([np.cos(phases), -np.sin(phases)]).astype(np.float32) / np.float32(math.sqrt(extent))
    high = tables.astype(BF16)
    low = (tables - high.astype(np.float32)).astype(BF16)
    return jnp.asarray(np.stack([high, low]))


def split(value):
    high = value.astype(BF16)
    return high, (value - high.astype(F32)).astype(BF16)


def product(left_op, right_op):
    dot = functools.partial(jnp.dot, preferred_element_type=F32)
    return dot(left_op[0], right_op[0]) + (dot(left_op[0], right_op[1]) + dot(left_op[1], right_op[0]))


def block_matrix(cos_part, sin_part):
    return jnp.concatenate(
        [jnp.concatenate([cos_part, sin_part], 1), jnp.concatenate([-sin_part, cos_part], 1)], 0
    )


def transform(fields, on_left, on_right):
    extent = fields[0][0].shape[0]
    stacked = jnp.concatenate(
        [jnp.concatenate([f[part] for f in fields], 1) for part in range(2)], 0
    )
    left = product(on_left, split(stacked))
    stacked = jnp.concatenate(
        [
            jnp.concatenate(
                [left[part * extent : (part + 1) * extent, m * extent : (m + 1) * extent] for part in range(2)], 1
            )
            for m in range(len(fields))
        ],
        0,
    )
    out = product(split(stacked), on_right)
    return [
        tuple(
            out[m * extent : (m + 1) * extent, part * extent : (part + 1) * extent] for part in range(2)
        )
        for m in range(len(fields))
    ]


def times(a, b):
    return (a[0] * b[0] - a[1] * b[1], a[0] * b[1] + a[1] * b[0])


def times_conj(a, b):
    return (a[0] * b[0] + a[1] * b[1], a[1] * b[0] - a[0] * b[1])


def placed(place_ref, first, extent):
    rows = pl.ds(pl.multiple_of(place_ref[first] * ROWS, ROWS), extent + ROWS)
    cols = pl.ds(pl.multiple_of(place_ref[first + 2] * extent, extent), 2 * extent)
    return rows, cols, place_ref[first + 1], place_ref[first + 3]


def wave_kernel(layers, place_ref, *refs):
    pieces, (probe_ref, prop_ref, measured_ref, table_ref, grad_ref, keep_ref, send_ref, frame_ref) = (
        refs[:-8],
        refs[-8:],
    )
    extent = probe_ref.shape[-1]
    mode_count = probe_ref.shape[0]
    tile_side = pieces[0].shape[-1]
    frame_ref[:, :, :tile_side, :tile_side] = pieces[0][...]
    frame_ref[:, :, :tile_side, tile_side:] = pieces[1][...]
    if len(pieces) > 2:
        below = pl.ds(tile_side, extent)
        frame_ref[:, :, below, :tile_side] = pieces[2][...]
        frame_ref[:, :, below, tile_side:] = pieces[3][...]
    rows, cols, row_shift, col_shift = placed(place_ref, 0, extent)

    def window(layer, part):
        wide = frame_ref[layer, part, rows, cols]
        tall = pltpu.roll(wide, lax.rem(2 * extent - col_shift, 2 * extent), 1)[:, :extent]
        return pltpu.roll(tall, lax.rem(extent + ROWS - row_shift, extent + ROWS), 0)[:extent]

    windows = [tuple(window(layer, part) for part in range(2)) for layer in range(layers)]
    probe = [tuple(probe_ref[m, part] for part in range(2)) for m in range(mode_count)]
    prop = (prop_ref[0], prop_ref[1])
    forward = tuple(block_matrix(table_ref[k, 0], table_ref[k, 1]) for k in range(2))
    backward = tuple(block_matrix(table_ref[k, 0], -table_ref[k, 1]) for k in range(2))

    fields = [times(p, windows[0]) for p in probe]
    entering = [probe]
    for layer in range(1, layers):
        fields = transform(fields, backward, forward)
        fields = [times(f, prop) for f in fields]
        fields = transform(fields, forward, backward)
        entering.append(fields)
        fields = [times(f, windows[layer]) for f in fields]
    fields = transform(fields, backward, forward)
    intensity = sum(f[0] * f[0] + f[1] * f[1] for f in fields)
    slope = (4.0 * LOSS_SCALE) * (intensity - measured_ref[...])
    fields = [(slope * f[0], slope * f[1]) for f in fields]
    fields = transform(fields, forward, backward)
    for layer in reversed(range(layers)):
        parts = [times_conj(f, e) for f, e in zip(fields, entering[layer])]
        for part in range(2):
            grad_ref[layer, part] = sum(p[part] for p in parts)
        fields = [times_conj(f, windows[layer]) for f in fields]
        if layer > 0:
            fields = transform(fields, backward, forward)
            fields = [times_conj(f, prop) for f in fields]
            fields = transform(fields, forward, backward)
    core = place_ref[4]
    for m in range(mode_count):
        keep_ref[m] = jnp.where(core == 0, fields[m][0], fields[m][1])
        send_ref[m] = jnp.where(core == 0, fields[m][1], fields[m][0])


VMEM = pl.BlockSpec(memory_space=pltpu.VMEM)
SMEM = pl.BlockSpec(memory_space=pltpu.SMEM)


def wave_gradients(place, pieces, probe, prop, measured, layers):
    extent = probe.shape[-1]
    tile_side = pieces[0].shape[-1]
    rows = tile_side + ROWS + (extent if len(pieces) > 2 else 0)
    return pl.pallas_call(
        functools.partial(wave_kernel, layers),
        out_shape=(
            jax.ShapeDtypeStruct((layers, 2, extent, extent), F32),
            jax.ShapeDtypeStruct((probe.shape[0], extent, extent), F32),
            jax.ShapeDtypeStruct((probe.shape[0], extent, extent), F32),
        ),
        in_specs=[SMEM] + [VMEM] * (len(pieces) + 4),
        out_specs=(VMEM, VMEM, VMEM),
        scratch_shapes=[pltpu.VMEM((layers, 2, rows, tile_side + extent), F32)],
        compiler_params=pltpu.CompilerParams(vmem_limit_bytes=24 << 20),
        name="wave_gradients",
    )(place, *pieces, probe, prop, measured, fourier_tables(extent))


def spread_kernel(count, place_ref, *refs):
    number = len(refs) - 1 - count
    windows, outs, frame_ref = refs[:number], refs[number:-1], refs[-1]
    extent = windows[0].shape[-1]
    frame_ref[...] = jnp.zeros_like(frame_ref)
    for w, window_ref in enumerate(windows):
        rows, cols, row_shift, col_shift = placed(place_ref, 5 * w, extent)
        for layer in range(window_ref.shape[0]):
            for part in range(2):
                block = jnp.concatenate([window_ref[layer, part], jnp.zeros((ROWS, extent), F32)], 0)
                block = pltpu.roll(block, row_shift, 0)
                wide = pltpu.roll(jnp.concatenate([block, jnp.zeros_like(block)], 1), col_shift, 1)
                at = (layer, part, rows, cols)
                frame_ref[at] = wide if w == 0 else wide + frame_ref[at]
    for k, out_ref in enumerate(outs):
        rows = out_ref.shape[2]
        first = pl.multiple_of(place_ref[5 * number + k] * rows, rows)
        out_ref[...] = frame_ref[:, :, pl.ds(first, rows), :]


def spread(place, windows, frame_rows, frame_cols, share_rows, count):
    layers = windows[0].shape[0]
    return pl.pallas_call(
        functools.partial(spread_kernel, count),
        out_shape=[jax.ShapeDtypeStruct((layers, 2, share_rows, frame_cols), F32)] * count,
        in_specs=[SMEM] + [VMEM] * len(windows),
        out_specs=[VMEM] * count,
        scratch_shapes=[pltpu.VMEM((layers, 2, frame_rows + ROWS, frame_cols), F32)],
        compiler_params=pltpu.CompilerParams(vmem_limit_bytes=24 << 20),
        name="spread_windows",
    )(place, *windows)


def local(object_slices, probe, prop_phase, scan_offsets, measured):
    own_tile = object_slices[0]
    layers = own_tile.shape[0]
    tile_side = own_tile.shape[-1]
    extent = probe.shape[-1]
    tiles = lax.axis_size("tile")
    shares = lax.axis_size("batch")
    tall = tiles > TGX
    share = lax.axis_index("batch")
    core = lax.rem(share, 2)
    half = tile_side // 2

    offset = scan_offsets[0, 0]
    place = jnp.stack([offset[0] // ROWS, offset[0] % ROWS, offset[1] // extent, offset[1] % extent, core])
    prop = jnp.stack([jnp.cos(prop_phase), jnp.sin(prop_phase)])
    strip = lax.dynamic_slice(own_tile, (0, 0, core * half, 0), (layers, 2, half, extent))
    strip = passed_along(strip, "tile", -1)
    other = exchanged(strip, "batch", 1)
    upper = jnp.where(core == 0, strip, other)
    lower = jnp.where(core == 0, other, strip)
    pieces = [own_tile, jnp.concatenate([upper, lower], 2)]
    if tall:
        pieces.append(passed_along(own_tile[:, :, :extent, :], "tile", -TGX))
        pieces.append(passed_along(own_tile[:, :, :extent, :extent], "tile", -TGX - 1))

    window_grad, probe_keep, probe_send = wave_gradients(
        place, pieces, probe, prop, measured[0, 0], layers
    )
    frame_cols = tile_side + extent
    if tall or shares != 4:
        frame_rows = tile_side + (extent if tall else 0)
        (frame,) = spread(
            jnp.concatenate([place, jnp.zeros((1,), jnp.int32)]),
            [window_grad], frame_rows, frame_cols, frame_rows, 1,
        )
        core_grad = frame[:, :, :tile_side, :tile_side]
        parts = [(1, frame[:, :, :tile_side, tile_side:])]
        if tall:
            parts.append((TGX, frame[:, :, tile_side:, :tile_side]))
            parts.append((TGX + 1, frame[:, :, tile_side:, tile_side:]))
        for distance, part in parts:
            landed = passed_along(part, "tile", distance)
            core_grad = core_grad.at[:, :, : landed.shape[2], : landed.shape[3]].add(landed)
        object_share = lax.psum_scatter(core_grad, "batch", scatter_dimension=2, tiled=True)
    else:
        place_across = exchanged(place, "batch", 2)
        across = exchanged(window_grad, "batch", 2)
        kept, given = spread(
            jnp.concatenate([place, place_across, jnp.stack([share, share ^ 1])]),
            [window_grad, across], tile_side, frame_cols, tile_side // shares, 2,
        )
        summed = kept + exchanged(given, "batch", 1)
        landed = passed_along(summed[:, :, :, tile_side:], "tile", 1)
        object_share = summed[:, :, :, :tile_side].at[:, :, :, :extent].add(landed)

    total = probe_keep + exchanged(probe_send, "batch", 1)
    for axis, size, first in (("batch", shares, 2), ("tile", tiles, 1)):
        bit = first
        while bit < size:
            total = total + exchanged(total, axis, bit)
            bit *= 2
    total = total / (tiles * shares)
    other = exchanged(total, "batch", 1)
    probe_step = jnp.stack([jnp.where(core == 0, total, other), jnp.where(core == 0, other, total)], 1)
    return (object_share[None], probe_step)


def solution(mesh):
    in_specs = (
        P("tile", None, None, None, None),
        P(),
        P(),
        P("tile", "batch", None),
        P("tile", "batch", None, None),
    )
    out_specs = (P("tile", None, None, "batch", None), P())
    return jax.shard_map(local, mesh=mesh, in_specs=in_specs, out_specs=out_specs, check_vma=False)
```

```python
import functools
import math

import jax
import jax.numpy as jnp
import numpy as np
from jax import lax
from jax.experimental import pallas as pl
from jax.experimental.pallas import tpu as pltpu
from jax.sharding import PartitionSpec as P

TGX = 8


LOSS_SCALE = 0.05

F32 = jnp.float32
BF16 = jnp.bfloat16
ROWS = 8


def passed_along(block, axis, distance):
    devices = range(lax.axis_size(axis))
    route = [(i - distance, i) for i in devices if i - distance in devices]
    return lax.ppermute(block, axis, route)


def exchanged(block, axis, bit):
    return lax.ppermute(block, axis, [(i, i ^ bit) for i in range(lax.axis_size(axis))])


def after(value, *others):
    return lax.optimization_barrier((value, *others))[0]


def fourier_tables(extent):
    indices = np.arange(extent)
    phases = (indices[:, None] * indices[None, :] % extent) * (2.0 * math.pi / extent)
    tables = np.stack([np.cos(phases), -np.sin(phases)]).astype(np.float32) / np.float32(math.sqrt(extent))
    high = tables.astype(BF16)
    low = (tables - high.astype(np.float32)).astype(BF16)
    return jnp.asarray(np.stack([high, low]))


def split(value):
    high = value.astype(BF16)
    return high, (value - high.astype(F32)).astype(BF16)


def product(left_op, right_op):
    dot = functools.partial(jnp.dot, preferred_element_type=F32)
    return dot(left_op[0], right_op[0]) + (dot(left_op[0], right_op[1]) + dot(left_op[1], right_op[0]))


def block_matrix(cos_part, sin_part):
    return jnp.concatenate(
        [jnp.concatenate([cos_part, sin_part], 1), jnp.concatenate([-sin_part, cos_part], 1)], 0
    )


def transform(fields, on_left, on_right):
    extent = fields[0][0].shape[0]
    stacked = jnp.concatenate(
        [jnp.concatenate([f[part] for f in fields], 1) for part in range(2)], 0
    )
    left = product(on_left, split(stacked))
    stacked = jnp.concatenate(
        [
            jnp.concatenate(
                [left[part * extent : (part + 1) * extent, m * extent : (m + 1) * extent] for part in range(2)], 1
            )
            for m in range(len(fields))
        ],
        0,
    )
    out = product(split(stacked), on_right)
    return [
        tuple(
            out[m * extent : (m + 1) * extent, part * extent : (part + 1) * extent] for part in range(2)
        )
        for m in range(len(fields))
    ]


def times(a, b):
    return (a[0] * b[0] - a[1] * b[1], a[0] * b[1] + a[1] * b[0])


def times_conj(a, b):
    return (a[0] * b[0] + a[1] * b[1], a[1] * b[0] - a[0] * b[1])


def rows_from(row, extent, tile_side):
    span = extent + ROWS
    first = jnp.minimum(row // ROWS * ROWS, tile_side - span)
    return pl.ds(pl.multiple_of(first, ROWS), span), row - first


def cut(wide, row, col, extent):
    rows, cols = wide.shape
    wide = pltpu.roll(wide, lax.rem(cols - col, cols), 1)[:, :extent]
    return pltpu.roll(wide, lax.rem(rows - row, rows), 0)[:extent]


def own_kernel(count, *refs):
    offset_refs = refs[:count]
    tile_ref, phase_ref, probe_in_ref, table_in_ref, own_ref, prop_ref, probe_ref, table_ref = refs[count:]
    extent = phase_ref.shape[-1]
    for p, offset_ref in enumerate(offset_refs):
        rows, shift = rows_from(offset_ref[0], extent, tile_ref.shape[-1])
        for layer in range(tile_ref.shape[0]):
            for part in range(2):
                own_ref[p, layer, part] = cut(tile_ref[layer, part, rows, :], shift, offset_ref[1], extent)
    prop_ref[0] = jnp.cos(phase_ref[...])
    prop_ref[1] = jnp.sin(phase_ref[...])
    probe_ref[...] = probe_in_ref[...]
    table_ref[...] = table_in_ref[...]


def whole_windows(offset_refs, core_ref, own_ref, first, pieces, strip_ref):
    mine_ref, other_ref = pieces[:2]
    layers, _, half, extent = mine_ref.shape
    tile_side = 2 * half
    core = core_ref[0]
    strip_ref[:, :, pl.ds(pl.multiple_of(core * half, half), half), :] = mine_ref[...]
    strip_ref[:, :, pl.ds(pl.multiple_of((1 - core) * half, half), half), :] = other_ref[...]

    def block(layer, part, p):
        row, col = offset_refs[p][0], offset_refs[p][1]
        rows, shift = rows_from(row, extent, tile_side)
        past_row = lax.broadcasted_iota(jnp.int32, (extent, extent), 0) >= tile_side - row
        past_col = lax.broadcasted_iota(jnp.int32, (extent, extent), 1) >= tile_side - col
        col_in = lax.rem(col, extent)
        row_in = lax.rem(row, extent)
        right = cut(strip_ref[layer, part, rows, :], shift, col_in, extent)
        value = jnp.where(past_col, right, own_ref[p, first + layer, part])
        if len(pieces) > 2:
            below = cut(pieces[2][layer, part], row_in, col, extent)
            corner = cut(pieces[3][layer, part], row_in, col_in, extent)
            value = jnp.where(past_row, jnp.where(past_col, corner, below), value)
        return value

    positions = range(len(offset_refs))
    return [[tuple(block(layer, part, p) for part in range(2)) for p in positions] for layer in range(layers)]


def wave_tools(probe_ref, prop_ref, table_ref):
    probe = [tuple(probe_ref[m, part] for part in range(2)) for m in range(probe_ref.shape[0])]
    prop = (prop_ref[0], prop_ref[1])
    forward = tuple(block_matrix(table_ref[k, 0], table_ref[k, 1]) for k in range(2))
    backward = tuple(block_matrix(table_ref[k, 0], -table_ref[k, 1]) for k in range(2))
    return probe, prop, forward, backward


def propagated(fields, prop, forward, backward):
    fields = transform(fields, backward, forward)
    fields = [times(f, prop) for f in fields]
    return transform(fields, forward, backward)


def enter_kernel(count, positions, *refs):
    offset_refs, core_ref = refs[:positions], refs[positions]
    own_ref, probe_ref, prop_ref, table_ref = refs[positions + 1 : positions + 5]
    pieces, (window_ref, wave_ref, strip_ref) = refs[positions + 5 : positions + 5 + count], refs[positions + 5 + count :]
    probe, prop, forward, backward = wave_tools(probe_ref, prop_ref, table_ref)
    (windows,) = whole_windows(offset_refs, core_ref, own_ref, 0, pieces, strip_ref)
    fields = propagated([times(p, w) for w in windows for p in probe], prop, forward, backward)
    for part in range(2):
        for p, window in enumerate(windows):
            window_ref[p, part] = window[part]
        for k, field in enumerate(fields):
            wave_ref[k, part] = field[part]


def wave_kernel(count, positions, *refs):
    offset_refs, core_ref = refs[:positions], refs[positions]
    own_ref, probe_ref, prop_ref, table_ref, window_ref, wave_ref = refs[positions + 1 : positions + 7]
    measured_refs = refs[positions + 7 : 2 * positions + 7]
    pieces = refs[2 * positions + 7 : 2 * positions + 7 + count]
    grad_ref, keep_ref, send_ref, strip_ref = refs[2 * positions + 7 + count :]
    layers = own_ref.shape[1]
    probe, prop, forward, backward = wave_tools(probe_ref, prop_ref, table_ref)
    modes = len(probe)
    windows = [[(window_ref[p, 0], window_ref[p, 1]) for p in range(positions)]]
    windows += whole_windows(offset_refs, core_ref, own_ref, 1, pieces, strip_ref)
    windows = [[w for w in layer for _ in range(modes)] for layer in windows]
    fields = [(wave_ref[k, 0], wave_ref[k, 1]) for k in range(positions * modes)]
    entering = [probe * positions]
    for layer in range(1, layers):
        if layer > 1:
            fields = propagated(fields, prop, forward, backward)
        entering.append(fields)
        fields = [times(f, w) for f, w in zip(fields, windows[layer])]
    fields = transform(fields, backward, forward)
    slopes = []
    for p in range(positions):
        intensity = sum(f[0] * f[0] + f[1] * f[1] for f in fields[p * modes : (p + 1) * modes])
        slopes += [(4.0 * LOSS_SCALE) * (intensity - measured_refs[p][...])] * modes
    fields = [(slope * f[0], slope * f[1]) for slope, f in zip(slopes, fields)]
    fields = transform(fields, forward, backward)
    for layer in reversed(range(layers)):
        parts = [times_conj(f, e) for f, e in zip(fields, entering[layer])]
        for p in range(positions):
            for part in range(2):
                grad_ref[p, layer, part] = sum(c[part] for c in parts[p * modes : (p + 1) * modes])
        fields = [times_conj(f, w) for f, w in zip(fields, windows[layer])]
        if layer > 0:
            fields = transform(fields, backward, forward)
            fields = [times_conj(f, prop) for f in fields]
            fields = transform(fields, forward, backward)
    core = core_ref[0]
    for m in range(modes):
        real, imag = (sum(fields[p * modes + m][part] for p in range(positions)) for part in range(2))
        keep_ref[m] = jnp.where(core == 0, real, imag)
        send_ref[m] = jnp.where(core == 0, imag, real)


VMEM = pl.BlockSpec(memory_space=pltpu.VMEM)
SMEM = pl.BlockSpec(memory_space=pltpu.SMEM)


def kernel_call(kernel, name, scalars, arrays, outs, scratch=(), flops=0):
    sizes = sum(math.prod(a.shape) * a.dtype.itemsize for a in arrays)
    return pl.pallas_call(
        kernel,
        out_shape=[jax.ShapeDtypeStruct(shape, dtype) for shape, dtype in outs],
        in_specs=[SMEM] * len(scalars) + [VMEM] * len(arrays),
        out_specs=[VMEM] * len(outs),
        scratch_shapes=[pltpu.VMEM(shape, F32) for shape in scratch],
        compiler_params=pltpu.CompilerParams(vmem_limit_bytes=24 << 20),
        cost_estimate=pl.CostEstimate(flops=flops, bytes_accessed=sizes, transcendentals=0),
        name=name,
    )(*scalars, *arrays)


def spread_kernel(shares, *refs):
    offset_refs, (share_ref, window_ref, keep_ref, send_ref, frame_ref) = refs[:-5], refs[-5:]
    extent = window_ref.shape[-1]
    frame_ref[...] = jnp.zeros_like(frame_ref)
    for p, offset_ref in enumerate(offset_refs):
        row, col = offset_ref[0], offset_ref[1]
        rows = pl.ds(pl.multiple_of(row // ROWS * ROWS, ROWS), extent + ROWS)
        cols = pl.ds(pl.multiple_of(col // extent * extent, extent), 2 * extent)
        for layer in range(window_ref.shape[1]):
            for part in range(2):
                block = jnp.concatenate([window_ref[p, layer, part], jnp.zeros((ROWS, extent), F32)], 0)
                block = pltpu.roll(block, lax.rem(row, ROWS), 0)
                wide = pltpu.roll(jnp.concatenate([block, jnp.zeros_like(block)], 1), lax.rem(col, extent), 1)
                at = (layer, part, rows, cols)
                frame_ref[at] = wide if p == 0 else wide + frame_ref[at]
    count = keep_ref.shape[2]
    for share, out_ref in ((share_ref[0], keep_ref), (share_ref[0] ^ 1, send_ref)):
        share = share if shares > 1 else 0
        out_ref[...] = frame_ref[:, :, pl.ds(pl.multiple_of(share * count, count), count), :]


def local(object_slices, probe, prop_phase, scan_offsets, measured):
    own_tile = object_slices[0]
    layers = own_tile.shape[0]
    tile_side = own_tile.shape[-1]
    extent = probe.shape[-1]
    tiles = lax.axis_size("tile")
    shares = lax.axis_size("batch")
    tall = tiles > TGX
    share = lax.axis_index("batch").reshape(1)
    core = share & 1
    half = tile_side // 2
    offset = scan_offsets[0, 0]
    table = fourier_tables(extent)

    def halo(first, count):
        strip = lax.dynamic_slice(own_tile, (first, 0, core[0] * half, 0), (count, 2, half, extent))
        strip = passed_along(strip, "tile", -1)
        if first == 0:
            strip = after(strip, own)
        pieces = [strip, exchanged(strip, "batch", 1)]
        if tall:
            rim = own_tile[first : first + count, :, :extent]
            pieces.append(passed_along(rim, "tile", -TGX))
            pieces.append(passed_along(rim[..., :extent], "tile", -TGX - 1))
        return pieces

    field = (extent, extent)
    paired = not tall and shares == 4
    offsets, targets = [offset], [measured[0, 0]]
    if paired:
        offsets.append(exchanged(offset, "batch", 2))
        targets.append(exchanged(measured[0, 0], "batch", 2))
    positions = len(offsets)
    own, prop, probe_in, table_in = kernel_call(
        functools.partial(own_kernel, positions), "own_windows", offsets, [own_tile, prop_phase, probe, table],
        [((positions, layers, 2) + field, F32), ((2,) + field, F32), (probe.shape, F32), (table.shape, BF16)],
    )
    if paired:
        own = after(own, targets[1])
    early = halo(0, 1)
    late = halo(1, layers - 1)
    shared = [own, probe_in, prop, table_in]
    window, wave = kernel_call(
        functools.partial(enter_kernel, len(early), positions), "entering_wave", offsets + [core], shared + early,
        [((positions, 2) + field, F32), ((positions * probe.shape[0], 2) + field, F32)],
        [(1, 2, tile_side, extent)],
    )
    window_grad, probe_keep, probe_send = kernel_call(
        functools.partial(wave_kernel, len(late), positions), "wave_gradients", offsets + [core],
        shared + [window, wave] + targets + late,
        [((positions, layers, 2) + field, F32), (probe.shape[:1] + field, F32), (probe.shape[:1] + field, F32)],
        [(layers - 1, 2, tile_side, extent)],
    )

    got = exchanged(probe_send, "batch", 1)
    cols = tile_side + extent
    rounds = [("batch", 1 << k) for k in range(1, (shares - 1).bit_length())]
    if paired:
        rounds = []
    rounds += [("tile", 1 << k) for k in range((tiles - 1).bit_length())]
    rows = tile_side + (extent if tall else 0)
    share_rows = tile_side // shares if paired else rows
    kept, given = kernel_call(
        functools.partial(spread_kernel, shares if paired else 1), "spread_windows", offsets + [share], [window_grad],
        [((layers, 2, share_rows, cols), F32)] * 2, [(layers, 2, rows + ROWS, cols)],
    )
    if paired:
        total = probe_keep + after(got, given)
        summed = kept + exchanged(given, "batch", 1)
        landed = passed_along(summed[:, :, :, tile_side:], "tile", 1)
        object_share = summed[:, :, :, :tile_side].at[:, :, :, :extent].add(landed)
        beside = [(summed,)]
    else:
        total = probe_keep + got
        core_grad = kept[:, :, :tile_side, :tile_side]
        parts = [(1, kept[:, :, :tile_side, tile_side:])]
        if tall:
            parts.append((TGX, kept[:, :, tile_side:, :tile_side]))
            parts.append((TGX + 1, kept[:, :, tile_side:, tile_side:]))
        for distance, part in parts:
            landed = passed_along(part, "tile", distance)
            core_grad = core_grad.at[:, :, : landed.shape[2], : landed.shape[3]].add(landed)
        object_share = lax.psum_scatter(core_grad, "batch", scatter_dimension=2, tiled=True)
        beside = []
    for k, (axis, bit) in enumerate(rounds):
        got = exchanged(total, axis, bit)
        total = total + (after(got, *beside[k]) if k < len(beside) else got)
    total = total / (tiles * shares)
    other = exchanged(total, "batch", 1)
    even = core[0] == 0
    probe_step = jnp.stack([jnp.where(even, total, other), jnp.where(even, other, total)], 1)
    return (object_share[None], probe_step)


def solution(mesh):
    in_specs = (
        P("tile", None, None, None, None),
        P(),
        P(),
        P("tile", "batch", None),
        P("tile", "batch", None, None),
    )
    out_specs = (P("tile", None, None, "batch", None), P())
    return jax.shard_map(local, mesh=mesh, in_specs=in_specs, out_specs=out_specs, check_vma=False)
```

```python
import functools
import math

import jax
import jax.numpy as jnp
import numpy as np
from jax import lax
from jax.experimental import pallas as pl
from jax.experimental.pallas import tpu as pltpu
from jax.sharding import PartitionSpec as P

TGX = 8


LOSS_SCALE = 0.05

F32 = jnp.float32
BF16 = jnp.bfloat16
ROWS = 8


def passed_along(block, axis, distance):
    devices = range(lax.axis_size(axis))
    route = [(i - distance, i) for i in devices if i - distance in devices]
    return lax.ppermute(block, axis, route)


def exchanged(block, axis, bit):
    return lax.ppermute(block, axis, [(i, i ^ bit) for i in range(lax.axis_size(axis))])


def after(value, *others):
    return lax.optimization_barrier((value, *others))[0]


def fourier_tables(extent):
    indices = np.arange(extent)
    phases = (indices[:, None] * indices[None, :] % extent) * (2.0 * math.pi / extent)
    tables = np.stack([np.cos(phases), -np.sin(phases)]).astype(np.float32) / np.float32(math.sqrt(extent))
    high = tables.astype(BF16)
    low = (tables - high.astype(np.float32)).astype(BF16)
    return jnp.asarray(np.stack([high, low]))


def split(value):
    high = value.astype(BF16)
    return high, (value - high.astype(F32)).astype(BF16)


def product(left_op, right_op):
    dot = functools.partial(jnp.dot, preferred_element_type=F32)
    return dot(left_op[0], right_op[0]) + (dot(left_op[0], right_op[1]) + dot(left_op[1], right_op[0]))


def block_matrix(cos_part, sin_part):
    return jnp.concatenate(
        [jnp.concatenate([cos_part, sin_part], 1), jnp.concatenate([-sin_part, cos_part], 1)], 0
    )


def transform(fields, on_left, on_right):
    extent = fields[0][0].shape[0]
    stacked = jnp.concatenate(
        [jnp.concatenate([f[part] for f in fields], 1) for part in range(2)], 0
    )
    left = product(on_left, split(stacked))
    stacked = jnp.concatenate(
        [
            jnp.concatenate(
                [left[part * extent : (part + 1) * extent, m * extent : (m + 1) * extent] for part in range(2)], 1
            )
            for m in range(len(fields))
        ],
        0,
    )
    out = product(split(stacked), on_right)
    return [
        tuple(
            out[m * extent : (m + 1) * extent, part * extent : (part + 1) * extent] for part in range(2)
        )
        for m in range(len(fields))
    ]


def times(a, b):
    return (a[0] * b[0] - a[1] * b[1], a[0] * b[1] + a[1] * b[0])


def times_conj(a, b):
    return (a[0] * b[0] + a[1] * b[1], a[1] * b[0] - a[0] * b[1])


def rows_from(row, extent, tile_side):
    span = extent + ROWS
    first = jnp.minimum(row // ROWS * ROWS, tile_side - span)
    return pl.ds(pl.multiple_of(first, ROWS), span), row - first


def cut(wide, row, col, extent):
    rows, cols = wide.shape
    wide = pltpu.roll(wide, lax.rem(cols - col, cols), 1)[:, :extent]
    return pltpu.roll(wide, lax.rem(rows - row, rows), 0)[:extent]


def own_windows(row, col, tile_ref, own_ref):
    extent = own_ref.shape[-1]
    rows, shift = rows_from(row, extent, tile_ref.shape[-1])
    for layer in range(tile_ref.shape[0]):
        for part in range(2):
            own_ref[layer, part] = cut(tile_ref[layer, part, rows, :], shift, col, extent)


def own_kernel(offset_ref, tile_ref, phase_ref, probe_in_ref, table_in_ref, own_ref, prop_ref, probe_ref, table_ref):
    own_windows(offset_ref[0], offset_ref[1], tile_ref, own_ref)
    prop_ref[0] = jnp.cos(phase_ref[...])
    prop_ref[1] = jnp.sin(phase_ref[...])
    probe_ref[...] = probe_in_ref[...]
    table_ref[...] = table_in_ref[...]


def partner_kernel(offset_ref, tile_ref, own_ref):
    own_windows(offset_ref[0], offset_ref[1], tile_ref, own_ref)


def whole_windows(offset_refs, core_ref, own_refs, first, pieces, strip_ref):
    mine_ref, other_ref = pieces[:2]
    layers, _, half, extent = mine_ref.shape
    tile_side = 2 * half
    core = core_ref[0]
    strip_ref[:, :, pl.ds(pl.multiple_of(core * half, half), half), :] = mine_ref[...]
    strip_ref[:, :, pl.ds(pl.multiple_of((1 - core) * half, half), half), :] = other_ref[...]

    def block(layer, part, p):
        row, col = offset_refs[p][0], offset_refs[p][1]
        rows, shift = rows_from(row, extent, tile_side)
        past_row = lax.broadcasted_iota(jnp.int32, (extent, extent), 0) >= tile_side - row
        past_col = lax.broadcasted_iota(jnp.int32, (extent, extent), 1) >= tile_side - col
        col_in = lax.rem(col, extent)
        row_in = lax.rem(row, extent)
        right = cut(strip_ref[layer, part, rows, :], shift, col_in, extent)
        value = jnp.where(past_col, right, own_refs[p][first + layer, part])
        if len(pieces) > 2:
            below = cut(pieces[2][layer, part], row_in, col, extent)
            corner = cut(pieces[3][layer, part], row_in, col_in, extent)
            value = jnp.where(past_row, jnp.where(past_col, corner, below), value)
        return value

    positions = range(len(offset_refs))
    return [[tuple(block(layer, part, p) for part in range(2)) for p in positions] for layer in range(layers)]


def wave_tools(probe_ref, prop_ref, table_ref):
    probe = [tuple(probe_ref[m, part] for part in range(2)) for m in range(probe_ref.shape[0])]
    prop = (prop_ref[0], prop_ref[1])
    forward = tuple(block_matrix(table_ref[k, 0], table_ref[k, 1]) for k in range(2))
    backward = tuple(block_matrix(table_ref[k, 0], -table_ref[k, 1]) for k in range(2))
    return probe, prop, forward, backward


def propagated(fields, prop, forward, backward):
    fields = transform(fields, backward, forward)
    fields = [times(f, prop) for f in fields]
    return transform(fields, forward, backward)


def enter_kernel(positions, *refs):
    offset_refs, core_ref = refs[:positions], refs[positions]
    own_refs, (probe_ref, prop_ref, table_ref) = refs[positions + 1 : 2 * positions + 1], refs[2 * positions + 1 :][:3]
    pieces, (window_ref, wave_ref, strip_ref) = refs[2 * positions + 4 : -3], refs[-3:]
    probe, prop, forward, backward = wave_tools(probe_ref, prop_ref, table_ref)
    (windows,) = whole_windows(offset_refs, core_ref, own_refs, 0, pieces, strip_ref)
    fields = propagated([times(p, w) for w in windows for p in probe], prop, forward, backward)
    for part in range(2):
        for p, window in enumerate(windows):
            window_ref[p, part] = window[part]
        for k, field in enumerate(fields):
            wave_ref[k, part] = field[part]


def wave_kernel(positions, *refs):
    offset_refs, core_ref = refs[:positions], refs[positions]
    own_refs, refs = refs[positions + 1 : 2 * positions + 1], refs[2 * positions + 1 :]
    probe_ref, prop_ref, table_ref, window_ref, wave_ref = refs[:5]
    measured_refs, pieces = refs[5 : 5 + positions], refs[5 + positions : -4]
    grad_ref, keep_ref, send_ref, strip_ref = refs[-4:]
    layers = own_refs[0].shape[0]
    probe, prop, forward, backward = wave_tools(probe_ref, prop_ref, table_ref)
    modes = len(probe)
    windows = [[(window_ref[p, 0], window_ref[p, 1]) for p in range(positions)]]
    windows += whole_windows(offset_refs, core_ref, own_refs, 1, pieces, strip_ref)
    windows = [[w for w in layer for _ in range(modes)] for layer in windows]
    fields = [(wave_ref[k, 0], wave_ref[k, 1]) for k in range(positions * modes)]
    entering = [probe * positions]
    for layer in range(1, layers):
        if layer > 1:
            fields = propagated(fields, prop, forward, backward)
        entering.append(fields)
        fields = [times(f, w) for f, w in zip(fields, windows[layer])]
    fields = transform(fields, backward, forward)
    slopes = []
    for p in range(positions):
        intensity = sum(f[0] * f[0] + f[1] * f[1] for f in fields[p * modes : (p + 1) * modes])
        slopes += [(4.0 * LOSS_SCALE) * (intensity - measured_refs[p][...])] * modes
    fields = [(slope * f[0], slope * f[1]) for slope, f in zip(slopes, fields)]
    fields = transform(fields, forward, backward)
    for layer in reversed(range(layers)):
        parts = [times_conj(f, e) for f, e in zip(fields, entering[layer])]
        for p in range(positions):
            for part in range(2):
                grad_ref[p, layer, part] = sum(c[part] for c in parts[p * modes : (p + 1) * modes])
        fields = [times_conj(f, w) for f, w in zip(fields, windows[layer])]
        if layer > 0:
            fields = transform(fields, backward, forward)
            fields = [times_conj(f, prop) for f in fields]
            fields = transform(fields, forward, backward)
    core = core_ref[0]
    for m in range(modes):
        real, imag = (sum(fields[p * modes + m][part] for p in range(positions)) for part in range(2))
        keep_ref[m] = jnp.where(core == 0, real, imag)
        send_ref[m] = jnp.where(core == 0, imag, real)


VMEM = pl.BlockSpec(memory_space=pltpu.VMEM)
SMEM = pl.BlockSpec(memory_space=pltpu.SMEM)


def kernel_call(kernel, name, scalars, arrays, outs, scratch=(), flops=0):
    sizes = sum(math.prod(a.shape) * a.dtype.itemsize for a in arrays)
    return pl.pallas_call(
        kernel,
        out_shape=[jax.ShapeDtypeStruct(shape, dtype) for shape, dtype in outs],
        in_specs=[SMEM] * len(scalars) + [VMEM] * len(arrays),
        out_specs=[SMEM if dtype == jnp.int32 else VMEM for _, dtype in outs],
        scratch_shapes=[pltpu.VMEM(shape, F32) for shape in scratch],
        compiler_params=pltpu.CompilerParams(vmem_limit_bytes=24 << 20),
        cost_estimate=pl.CostEstimate(flops=flops, bytes_accessed=sizes, transcendentals=0),
        name=name,
    )(*scalars, *arrays)


def spread_kernel(shares, *refs):
    offset_refs, (share_ref, window_ref, keep_ref, send_ref, frame_ref) = refs[:-5], refs[-5:]
    extent = window_ref.shape[-1]
    frame_ref[...] = jnp.zeros_like(frame_ref)
    for p, offset_ref in enumerate(offset_refs):
        row, col = offset_ref[0], offset_ref[1]
        rows = pl.ds(pl.multiple_of(row // ROWS * ROWS, ROWS), extent + ROWS)
        cols = pl.ds(pl.multiple_of(col // extent * extent, extent), 2 * extent)
        for layer in range(window_ref.shape[1]):
            for part in range(2):
                block = jnp.concatenate([window_ref[p, layer, part], jnp.zeros((ROWS, extent), F32)], 0)
                block = pltpu.roll(block, lax.rem(row, ROWS), 0)
                wide = pltpu.roll(jnp.concatenate([block, jnp.zeros_like(block)], 1), lax.rem(col, extent), 1)
                at = (layer, part, rows, cols)
                frame_ref[at] = wide if p == 0 else wide + frame_ref[at]
    count = keep_ref.shape[2]
    for share, out_ref in ((share_ref[0], keep_ref), (share_ref[0] ^ 1, send_ref)):
        share = share if shares > 1 else 0
        out_ref[...] = frame_ref[:, :, pl.ds(pl.multiple_of(share * count, count), count), :]


def local(object_slices, probe, prop_phase, scan_offsets, measured):
    own_tile = object_slices[0]
    layers = own_tile.shape[0]
    tile_side = own_tile.shape[-1]
    extent = probe.shape[-1]
    tiles = lax.axis_size("tile")
    shares = lax.axis_size("batch")
    tall = tiles > TGX
    share = lax.axis_index("batch").reshape(1)
    core = share & 1
    half = tile_side // 2
    offset = scan_offsets[0, 0]
    table = fourier_tables(extent)

    def halo(first, count):
        strip = lax.dynamic_slice(own_tile, (first, 0, core[0] * half, 0), (count, 2, half, extent))
        strip = passed_along(strip, "tile", -1)
        if first == 0:
            strip = after(strip, *owns)
        pieces = [strip, exchanged(strip, "batch", 1)]
        if tall:
            rim = own_tile[first : first + count, :, :extent]
            pieces.append(passed_along(rim, "tile", -TGX))
            pieces.append(passed_along(rim[..., :extent], "tile", -TGX - 1))
        return pieces

    field = (extent, extent)
    paired = not tall and shares == 4
    offsets, targets = [offset], [measured[0, 0]]
    own, prop, probe_in, table_in = kernel_call(
        own_kernel, "own_windows", offsets, [own_tile, prop_phase, probe, table],
        [((layers, 2) + field, F32), ((2,) + field, F32), (probe.shape, F32), (table.shape, BF16)],
    )
    owns = [own]
    if paired:
        offsets.append(after(exchanged(offset, "batch", 2), own))
        (partner_own,) = kernel_call(
            partner_kernel, "partner_windows", [offsets[1]], [own_tile], [((layers, 2) + field, F32)]
        )
        owns.append(partner_own)
    positions = len(offsets)
    early = halo(0, 1)
    late = halo(1, layers - 1)
    if paired:
        targets.append(exchanged(after(measured[0, 0], early[0]), "batch", 2))
    shared = owns + [probe_in, prop, table_in]
    window, wave = kernel_call(
        functools.partial(enter_kernel, positions), "entering_wave", offsets + [core], shared + early,
        [((positions, 2) + field, F32), ((positions * probe.shape[0], 2) + field, F32)],
        [(1, 2, tile_side, extent)],
    )
    window_grad, probe_keep, probe_send = kernel_call(
        functools.partial(wave_kernel, positions), "wave_gradients", offsets + [core],
        shared + [window, wave] + targets + late,
        [((positions, layers, 2) + field, F32), (probe.shape[:1] + field, F32), (probe.shape[:1] + field, F32)],
        [(layers - 1, 2, tile_side, extent)],
    )

    got = exchanged(probe_send, "batch", 1)
    cols = tile_side + extent
    rounds = [("batch", 1 << k) for k in range(1, (shares - 1).bit_length())]
    if paired:
        rounds = []
    rounds += [("tile", 1 << k) for k in range((tiles - 1).bit_length())]
    frame_rows = tile_side + (extent if tall else 0)
    share_rows = tile_side // shares if paired else frame_rows
    kept, given = kernel_call(
        functools.partial(spread_kernel, shares if paired else 1), "spread_windows", offsets + [share], [window_grad],
        [((layers, 2, share_rows, cols), F32)] * 2, [(layers, 2, frame_rows + ROWS, cols)],
    )
    if paired:
        total = probe_keep + after(got, given)
        summed = kept + exchanged(given, "batch", 1)
        landed = passed_along(summed[:, :, :, tile_side:], "tile", 1)
        object_share = summed[:, :, :, :tile_side].at[:, :, :, :extent].add(landed)
        beside = [(summed,)]
    else:
        total = probe_keep + got
        core_grad = kept[:, :, :tile_side, :tile_side]
        parts = [(1, kept[:, :, :tile_side, tile_side:])]
        if tall:
            parts.append((TGX, kept[:, :, tile_side:, :tile_side]))
            parts.append((TGX + 1, kept[:, :, tile_side:, tile_side:]))
        for distance, part in parts:
            landed = passed_along(part, "tile", distance)
            core_grad = core_grad.at[:, :, : landed.shape[2], : landed.shape[3]].add(landed)
        object_share = lax.psum_scatter(core_grad, "batch", scatter_dimension=2, tiled=True)
        beside = []
    for k, (axis, bit) in enumerate(rounds):
        got = exchanged(total, axis, bit)
        total = total + (after(got, *beside[k]) if k < len(beside) else got)
    total = total / (tiles * shares)
    other = exchanged(total, "batch", 1)
    even = core[0] == 0
    probe_step = jnp.stack([jnp.where(even, total, other), jnp.where(even, other, total)], 1)
    return (object_share[None], probe_step)


def solution(mesh):
    in_specs = (
        P("tile", None, None, None, None),
        P(),
        P(),
        P("tile", "batch", None),
        P("tile", "batch", None, None),
    )
    out_specs = (P("tile", None, None, "batch", None), P())
    return jax.shard_map(local, mesh=mesh, in_specs=in_specs, out_specs=out_specs, check_vma=False)
```

```python
import functools
import math

import jax
import jax.numpy as jnp
import numpy as np
from jax import lax
from jax.experimental import pallas as pl
from jax.experimental.pallas import tpu as pltpu
from jax.sharding import PartitionSpec as P

TGX = 8


LOSS_SCALE = 0.05

F32 = jnp.float32
BF16 = jnp.bfloat16
ROWS = 8


def passed_along(block, axis, distance):
    devices = range(lax.axis_size(axis))
    route = [(i - distance, i) for i in devices if i - distance in devices]
    return lax.ppermute(block, axis, route)


def exchanged(block, axis, bit):
    return lax.ppermute(block, axis, [(i, i ^ bit) for i in range(lax.axis_size(axis))])


def after(value, *others):
    return lax.optimization_barrier((value, *others))[0]


def fourier_tables(extent):
    indices = np.arange(extent)
    phases = (indices[:, None] * indices[None, :] % extent) * (2.0 * math.pi / extent)
    tables = np.stack([np.cos(phases), -np.sin(phases)]).astype(np.float32) / np.float32(math.sqrt(extent))
    high = tables.astype(BF16)
    low = (tables - high.astype(np.float32)).astype(BF16)
    return jnp.asarray(np.stack([high, low]))


def split(value):
    high = value.astype(BF16)
    return high, (value - high.astype(F32)).astype(BF16)


def product(left_op, right_op):
    dot = functools.partial(jnp.dot, preferred_element_type=F32)
    return dot(left_op[0], right_op[0]) + (dot(left_op[0], right_op[1]) + dot(left_op[1], right_op[0]))


def block_matrix(cos_part, sin_part):
    return jnp.concatenate(
        [jnp.concatenate([cos_part, sin_part], 1), jnp.concatenate([-sin_part, cos_part], 1)], 0
    )


def transform(fields, on_left, on_right):
    extent = fields[0][0].shape[0]
    stacked = jnp.concatenate(
        [jnp.concatenate([f[part] for f in fields], 1) for part in range(2)], 0
    )
    left = product(on_left, split(stacked))
    stacked = jnp.concatenate(
        [
            jnp.concatenate(
                [left[part * extent : (part + 1) * extent, m * extent : (m + 1) * extent] for part in range(2)], 1
            )
            for m in range(len(fields))
        ],
        0,
    )
    out = product(split(stacked), on_right)
    return [
        tuple(
            out[m * extent : (m + 1) * extent, part * extent : (part + 1) * extent] for part in range(2)
        )
        for m in range(len(fields))
    ]


def times(a, b):
    return (a[0] * b[0] - a[1] * b[1], a[0] * b[1] + a[1] * b[0])


def times_conj(a, b):
    return (a[0] * b[0] + a[1] * b[1], a[1] * b[0] - a[0] * b[1])


def rows_from(row, extent, tile_side):
    span = extent + ROWS
    first = jnp.minimum(row // ROWS * ROWS, tile_side - span)
    return pl.ds(pl.multiple_of(first, ROWS), span), row - first


def cut(wide, row, col, extent):
    rows, cols = wide.shape
    wide = pltpu.roll(wide, lax.rem(cols - col, cols), 1)[:, :extent]
    return pltpu.roll(wide, lax.rem(rows - row, rows), 0)[:extent]


def own_windows(row, col, tile_ref, own_ref):
    extent = own_ref.shape[-1]
    rows, shift = rows_from(row, extent, tile_ref.shape[-1])
    for layer in range(tile_ref.shape[0]):
        for part in range(2):
            own_ref[layer, part] = cut(tile_ref[layer, part, rows, :], shift, col, extent)


def own_kernel(offset_ref, tile_ref, phase_ref, probe_in_ref, table_in_ref, own_ref, prop_ref, probe_ref, table_ref):
    own_windows(offset_ref[0], offset_ref[1], tile_ref, own_ref)
    prop_ref[0] = jnp.cos(phase_ref[...])
    prop_ref[1] = jnp.sin(phase_ref[...])
    probe_ref[...] = probe_in_ref[...]
    table_ref[...] = table_in_ref[...]


def partner_kernel(offset_ref, tile_ref, own_ref):
    own_windows(offset_ref[0], offset_ref[1], tile_ref, own_ref)


def whole_windows(offset_refs, core_ref, own_refs, pieces, strip_ref):
    mine_ref, other_ref = pieces[:2]
    layers, _, half, extent = mine_ref.shape
    tile_side = 2 * half
    core = core_ref[0]
    strip_ref[:, :, pl.ds(pl.multiple_of(core * half, half), half), :] = mine_ref[...]
    strip_ref[:, :, pl.ds(pl.multiple_of((1 - core) * half, half), half), :] = other_ref[...]

    def block(layer, part, p):
        row, col = offset_refs[p][0], offset_refs[p][1]
        rows, shift = rows_from(row, extent, tile_side)
        past_row = lax.broadcasted_iota(jnp.int32, (extent, extent), 0) >= tile_side - row
        past_col = lax.broadcasted_iota(jnp.int32, (extent, extent), 1) >= tile_side - col
        col_in = lax.rem(col, extent)
        row_in = lax.rem(row, extent)
        right = cut(strip_ref[layer, part, rows, :], shift, col_in, extent)
        value = jnp.where(past_col, right, own_refs[p][layer, part])
        if len(pieces) > 2:
            below = cut(pieces[2][layer, part], row_in, col, extent)
            corner = cut(pieces[3][layer, part], row_in, col_in, extent)
            value = jnp.where(past_row, jnp.where(past_col, corner, below), value)
        return value

    positions = range(len(offset_refs))
    return [[tuple(block(layer, part, p) for part in range(2)) for p in positions] for layer in range(layers)]


def wave_tools(probe_ref, prop_ref, table_ref):
    probe = [tuple(probe_ref[m, part] for part in range(2)) for m in range(probe_ref.shape[0])]
    prop = (prop_ref[0], prop_ref[1])
    forward = tuple(block_matrix(table_ref[k, 0], table_ref[k, 1]) for k in range(2))
    backward = tuple(block_matrix(table_ref[k, 0], -table_ref[k, 1]) for k in range(2))
    return probe, prop, forward, backward


def propagated(fields, prop, forward, backward):
    fields = transform(fields, backward, forward)
    fields = [times(f, prop) for f in fields]
    return transform(fields, forward, backward)


def wave_kernel(positions, *refs):
    offset_refs, core_ref = refs[:positions], refs[positions]
    own_refs, refs = refs[positions + 1 : 2 * positions + 1], refs[2 * positions + 1 :]
    probe_ref, prop_ref, table_ref = refs[:3]
    measured_refs, pieces = refs[3 : 3 + positions], refs[3 + positions : -4]
    grad_ref, keep_ref, send_ref, strip_ref = refs[-4:]
    layers = own_refs[0].shape[0]
    probe, prop, forward, backward = wave_tools(probe_ref, prop_ref, table_ref)
    modes = len(probe)
    windows = whole_windows(offset_refs, core_ref, own_refs, pieces, strip_ref)
    windows = [[w for w in layer for _ in range(modes)] for layer in windows]
    fields = probe * positions
    entering = []
    for layer in range(layers):
        if layer > 0:
            fields = propagated(fields, prop, forward, backward)
        entering.append(fields)
        fields = [times(f, w) for f, w in zip(fields, windows[layer])]
    fields = transform(fields, backward, forward)
    slopes = []
    for p in range(positions):
        intensity = sum(f[0] * f[0] + f[1] * f[1] for f in fields[p * modes : (p + 1) * modes])
        slopes += [(4.0 * LOSS_SCALE) * (intensity - measured_refs[p][...])] * modes
    fields = [(slope * f[0], slope * f[1]) for slope, f in zip(slopes, fields)]
    fields = transform(fields, forward, backward)
    for layer in reversed(range(layers)):
        parts = [times_conj(f, e) for f, e in zip(fields, entering[layer])]
        for p in range(positions):
            for part in range(2):
                grad_ref[p, layer, part] = sum(c[part] for c in parts[p * modes : (p + 1) * modes])
        fields = [times_conj(f, w) for f, w in zip(fields, windows[layer])]
        if layer > 0:
            fields = transform(fields, backward, forward)
            fields = [times_conj(f, prop) for f in fields]
            fields = transform(fields, forward, backward)
    core = core_ref[0]
    for m in range(modes):
        real, imag = (sum(fields[p * modes + m][part] for p in range(positions)) for part in range(2))
        keep_ref[m] = jnp.where(core == 0, real, imag)
        send_ref[m] = jnp.where(core == 0, imag, real)


VMEM = pl.BlockSpec(memory_space=pltpu.VMEM)
SMEM = pl.BlockSpec(memory_space=pltpu.SMEM)


def kernel_call(kernel, name, scalars, arrays, outs, scratch=(), flops=0):
    sizes = sum(math.prod(a.shape) * a.dtype.itemsize for a in arrays)
    return pl.pallas_call(
        kernel,
        out_shape=[jax.ShapeDtypeStruct(shape, dtype) for shape, dtype in outs],
        in_specs=[SMEM] * len(scalars) + [VMEM] * len(arrays),
        out_specs=[SMEM if dtype == jnp.int32 else VMEM for _, dtype in outs],
        scratch_shapes=[pltpu.VMEM(shape, F32) for shape in scratch],
        compiler_params=pltpu.CompilerParams(vmem_limit_bytes=24 << 20),
        cost_estimate=pl.CostEstimate(flops=flops, bytes_accessed=sizes, transcendentals=0),
        name=name,
    )(*scalars, *arrays)


def spread_kernel(shares, *refs):
    offset_refs, (share_ref, window_ref, keep_ref, send_ref, frame_ref) = refs[:-5], refs[-5:]
    extent = window_ref.shape[-1]
    frame_ref[...] = jnp.zeros_like(frame_ref)
    for p, offset_ref in enumerate(offset_refs):
        row, col = offset_ref[0], offset_ref[1]
        rows = pl.ds(pl.multiple_of(row // ROWS * ROWS, ROWS), extent + ROWS)
        cols = pl.ds(pl.multiple_of(col // extent * extent, extent), 2 * extent)
        for layer in range(window_ref.shape[1]):
            for part in range(2):
                block = jnp.concatenate([window_ref[p, layer, part], jnp.zeros((ROWS, extent), F32)], 0)
                block = pltpu.roll(block, lax.rem(row, ROWS), 0)
                wide = pltpu.roll(jnp.concatenate([block, jnp.zeros_like(block)], 1), lax.rem(col, extent), 1)
                at = (layer, part, rows, cols)
                frame_ref[at] = wide if p == 0 else wide + frame_ref[at]
    count = keep_ref.shape[2]
    for share, out_ref in ((share_ref[0], keep_ref), (share_ref[0] ^ 1, send_ref)):
        share = share if shares > 1 else 0
        out_ref[...] = frame_ref[:, :, pl.ds(pl.multiple_of(share * count, count), count), :]


def local(object_slices, probe, prop_phase, scan_offsets, measured):
    own_tile = object_slices[0]
    layers = own_tile.shape[0]
    tile_side = own_tile.shape[-1]
    extent = probe.shape[-1]
    tiles = lax.axis_size("tile")
    shares = lax.axis_size("batch")
    tall = tiles > TGX
    share = lax.axis_index("batch").reshape(1)
    core = share & 1
    half = tile_side // 2
    offset = scan_offsets[0, 0]
    table = fourier_tables(extent)

    field = (extent, extent)
    paired = not tall and shares == 4
    offsets, targets = [offset], [measured[0, 0]]
    own, prop, probe_in, table_in = kernel_call(
        own_kernel, "own_windows", offsets, [own_tile, prop_phase, probe, table],
        [((layers, 2) + field, F32), ((2,) + field, F32), (probe.shape, F32), (table.shape, BF16)],
    )
    owns = [own]
    if paired:
        offsets.append(after(exchanged(offset, "batch", 2), own))
        (partner_own,) = kernel_call(
            partner_kernel, "partner_windows", [offsets[1]], [own_tile], [((layers, 2) + field, F32)]
        )
        owns.append(partner_own)
        targets.append(exchanged(measured[0, 0], "batch", 2))
    positions = len(offsets)
    strip = lax.dynamic_slice(own_tile, (0, 0, core[0] * half, 0), (layers, 2, half, extent))
    strip = after(passed_along(strip, "tile", -1), *owns, *targets)
    pieces = [strip, exchanged(strip, "batch", 1)]
    if tall:
        rim = own_tile[:, :, :extent]
        pieces.append(passed_along(rim, "tile", -TGX))
        pieces.append(passed_along(rim[..., :extent], "tile", -TGX - 1))
    window_grad, probe_keep, probe_send = kernel_call(
        functools.partial(wave_kernel, positions), "wave_gradients", offsets + [core],
        owns + [probe_in, prop, table_in] + targets + pieces,
        [((positions, layers, 2) + field, F32), (probe.shape[:1] + field, F32), (probe.shape[:1] + field, F32)],
        [(layers, 2, tile_side, extent)],
    )

    got = exchanged(probe_send, "batch", 1)
    cols = tile_side + extent
    rounds = [("batch", 1 << k) for k in range(1, (shares - 1).bit_length())]
    if paired:
        rounds = []
    rounds += [("tile", 1 << k) for k in range((tiles - 1).bit_length())]
    frame_rows = tile_side + (extent if tall else 0)
    share_rows = tile_side // shares if paired else frame_rows
    kept, given = kernel_call(
        functools.partial(spread_kernel, shares if paired else 1), "spread_windows", offsets + [share], [window_grad],
        [((layers, 2, share_rows, cols), F32)] * 2, [(layers, 2, frame_rows + ROWS, cols)],
    )
    if paired:
        total = probe_keep + after(got, given)
        summed = kept + exchanged(given, "batch", 1)
        landed = passed_along(summed[:, :, :, tile_side:], "tile", 1)
        object_share = summed[:, :, :, :tile_side].at[:, :, :, :extent].add(landed)
        beside = [(summed,)]
    else:
        total = probe_keep + got
        core_grad = kept[:, :, :tile_side, :tile_side]
        parts = [(1, kept[:, :, :tile_side, tile_side:])]
        if tall:
            parts.append((TGX, kept[:, :, tile_side:, :tile_side]))
            parts.append((TGX + 1, kept[:, :, tile_side:, tile_side:]))
        for distance, part in parts:
            landed = passed_along(part, "tile", distance)
            core_grad = core_grad.at[:, :, : landed.shape[2], : landed.shape[3]].add(landed)
        object_share = lax.psum_scatter(core_grad, "batch", scatter_dimension=2, tiled=True)
        beside = []
    for k, (axis, bit) in enumerate(rounds):
        got = exchanged(total, axis, bit)
        total = total + (after(got, *beside[k]) if k < len(beside) else got)
    total = total / (tiles * shares)
    other = exchanged(total, "batch", 1)
    even = core[0] == 0
    probe_step = jnp.stack([jnp.where(even, total, other), jnp.where(even, other, total)], 1)
    return (object_share[None], probe_step)


def solution(mesh):
    in_specs = (
        P("tile", None, None, None, None),
        P(),
        P(),
        P("tile", "batch", None),
        P("tile", "batch", None, None),
    )
    out_specs = (P("tile", None, None, "batch", None), P())
    return jax.shard_map(local, mesh=mesh, in_specs=in_specs, out_specs=out_specs, check_vma=False)
```

```python
import functools
import math

import jax
import jax.numpy as jnp
import numpy as np
from jax import lax
from jax.experimental import pallas as pl
from jax.experimental.pallas import tpu as pltpu
from jax.sharding import PartitionSpec as P

TGX = 8


LOSS_SCALE = 0.05

F32 = jnp.float32
BF16 = jnp.bfloat16
ROWS = 8


def passed_along(block, axis, distance):
    devices = range(lax.axis_size(axis))
    route = [(i - distance, i) for i in devices if i - distance in devices]
    return lax.ppermute(block, axis, route)


def exchanged(block, axis, bit):
    return lax.ppermute(block, axis, [(i, i ^ bit) for i in range(lax.axis_size(axis))])


def after(value, *others):
    return lax.optimization_barrier((value, *others))[0]


def fourier_tables(extent):
    indices = np.arange(extent)
    phases = (indices[:, None] * indices[None, :] % extent) * (2.0 * math.pi / extent)
    tables = np.stack([np.cos(phases), -np.sin(phases)]).astype(np.float32) / np.float32(math.sqrt(extent))
    high = tables.astype(BF16)
    low = (tables - high.astype(np.float32)).astype(BF16)
    return jnp.asarray(np.stack([high, low]))


def split(value):
    high = value.astype(BF16)
    return high, (value - high.astype(F32)).astype(BF16)


def product(left_op, right_op):
    dot = functools.partial(jnp.dot, preferred_element_type=F32)
    return dot(left_op[0], right_op[0]) + (dot(left_op[0], right_op[1]) + dot(left_op[1], right_op[0]))


def block_matrix(cos_part, sin_part):
    return jnp.concatenate(
        [jnp.concatenate([cos_part, sin_part], 1), jnp.concatenate([-sin_part, cos_part], 1)], 0
    )


def transform(fields, on_left, on_right):
    extent = fields[0][0].shape[0]
    stacked = jnp.concatenate(
        [jnp.concatenate([f[part] for f in fields], 1) for part in range(2)], 0
    )
    left = product(on_left, split(stacked))
    stacked = jnp.concatenate(
        [
            jnp.concatenate(
                [left[part * extent : (part + 1) * extent, m * extent : (m + 1) * extent] for part in range(2)], 1
            )
            for m in range(len(fields))
        ],
        0,
    )
    out = product(split(stacked), on_right)
    return [
        tuple(
            out[m * extent : (m + 1) * extent, part * extent : (part + 1) * extent] for part in range(2)
        )
        for m in range(len(fields))
    ]


def times(a, b):
    return (a[0] * b[0] - a[1] * b[1], a[0] * b[1] + a[1] * b[0])


def times_conj(a, b):
    return (a[0] * b[0] + a[1] * b[1], a[1] * b[0] - a[0] * b[1])


def rows_from(row, extent, tile_side):
    span = extent + ROWS
    first = jnp.minimum(row // ROWS * ROWS, tile_side - span)
    return pl.ds(pl.multiple_of(first, ROWS), span), row - first


def cut(wide, row, col, extent):
    rows, cols = wide.shape
    wide = pltpu.roll(wide, lax.rem(cols - col, cols), 1)[:, :extent]
    return pltpu.roll(wide, lax.rem(rows - row, rows), 0)[:extent]


def own_windows(row, col, tile_ref, own_ref):
    extent = own_ref.shape[-1]
    rows, shift = rows_from(row, extent, tile_ref.shape[-1])
    for layer in range(tile_ref.shape[0]):
        for part in range(2):
            own_ref[layer, part] = cut(tile_ref[layer, part, rows, :], shift, col, extent)


def own_kernel(offset_ref, tile_ref, phase_ref, probe_in_ref, table_in_ref, own_ref, prop_ref, probe_ref, table_ref):
    own_windows(offset_ref[0], offset_ref[1], tile_ref, own_ref)
    prop_ref[0] = jnp.cos(phase_ref[...])
    prop_ref[1] = jnp.sin(phase_ref[...])
    probe_ref[...] = probe_in_ref[...]
    table_ref[...] = table_in_ref[...]


def partner_kernel(offset_ref, tile_ref, own_ref):
    own_windows(offset_ref[0], offset_ref[1], tile_ref, own_ref)


def whole_windows(offset_refs, core_ref, own_refs, pieces, strip_ref):
    mine_ref, other_ref = pieces[:2]
    layers, _, half, extent = mine_ref.shape
    tile_side = 2 * half
    core = core_ref[0]
    strip_ref[:, :, pl.ds(pl.multiple_of(core * half, half), half), :] = mine_ref[...]
    strip_ref[:, :, pl.ds(pl.multiple_of((1 - core) * half, half), half), :] = other_ref[...]

    def block(layer, part, p):
        row, col = offset_refs[p][0], offset_refs[p][1]
        rows, shift = rows_from(row, extent, tile_side)
        past_row = lax.broadcasted_iota(jnp.int32, (extent, extent), 0) >= tile_side - row
        past_col = lax.broadcasted_iota(jnp.int32, (extent, extent), 1) >= tile_side - col
        col_in = lax.rem(col, extent)
        row_in = lax.rem(row, extent)
        right = cut(strip_ref[layer, part, rows, :], shift, col_in, extent)
        value = jnp.where(past_col, right, own_refs[p][layer, part])
        if len(pieces) > 2:
            below = cut(pieces[2][layer, part], row_in, col, extent)
            corner = cut(pieces[3][layer, part], row_in, col_in, extent)
            value = jnp.where(past_row, jnp.where(past_col, corner, below), value)
        return value

    positions = range(len(offset_refs))
    return [[tuple(block(layer, part, p) for part in range(2)) for p in positions] for layer in range(layers)]


def wave_tools(probe_ref, prop_ref, table_ref):
    probe = [tuple(probe_ref[m, part] for part in range(2)) for m in range(probe_ref.shape[0])]
    prop = (prop_ref[0], prop_ref[1])
    forward = tuple(block_matrix(table_ref[k, 0], table_ref[k, 1]) for k in range(2))
    backward = tuple(block_matrix(table_ref[k, 0], -table_ref[k, 1]) for k in range(2))
    return probe, prop, forward, backward


def propagated(fields, prop, forward, backward):
    fields = transform(fields, backward, forward)
    fields = [times(f, prop) for f in fields]
    return transform(fields, forward, backward)


def wave_kernel(positions, *refs):
    offset_refs, core_ref = refs[:positions], refs[positions]
    own_refs, refs = refs[positions + 1 : 2 * positions + 1], refs[2 * positions + 1 :]
    probe_ref, prop_ref, table_ref = refs[:3]
    measured_refs, pieces = refs[3 : 3 + positions], refs[3 + positions : -6]
    kept_ref, given_ref, keep_ref, send_ref, strip_ref, frame_ref = refs[-6:]
    frame_ref[...] = jnp.zeros_like(frame_ref)
    layers = own_refs[0].shape[0]
    probe, prop, forward, backward = wave_tools(probe_ref, prop_ref, table_ref)
    modes = len(probe)
    windows = whole_windows(offset_refs, core_ref, own_refs, pieces, strip_ref)
    windows = [[w for w in layer for _ in range(modes)] for layer in windows]
    fields = probe * positions
    entering = []
    for layer in range(layers):
        if layer > 0:
            fields = propagated(fields, prop, forward, backward)
        entering.append(fields)
        fields = [times(f, w) for f, w in zip(fields, windows[layer])]
    fields = transform(fields, backward, forward)
    slopes = []
    for p in range(positions):
        intensity = sum(f[0] * f[0] + f[1] * f[1] for f in fields[p * modes : (p + 1) * modes])
        slopes += [(4.0 * LOSS_SCALE) * (intensity - measured_refs[p][...])] * modes
    fields = [(slope * f[0], slope * f[1]) for slope, f in zip(slopes, fields)]
    fields = transform(fields, forward, backward)
    for layer in reversed(range(layers)):
        parts = [times_conj(f, e) for f, e in zip(fields, entering[layer])]
        for p in range(positions):
            for part in range(2):
                block = sum(c[part] for c in parts[p * modes : (p + 1) * modes])
                lay(frame_ref, layer, part, offset_refs[p], block, p == 0)
        fields = [times_conj(f, w) for f, w in zip(fields, windows[layer])]
        if layer > 0:
            fields = transform(fields, backward, forward)
            fields = [times_conj(f, prop) for f in fields]
            fields = transform(fields, forward, backward)
    core = core_ref[0]
    count = kept_ref.shape[2]
    for share, out_ref in ((core_ref[1], kept_ref), (core_ref[1] ^ 1, given_ref)):
        share = share if positions > 1 else 0
        out_ref[...] = frame_ref[:, :, pl.ds(pl.multiple_of(share * count, count), count), :]
    for m in range(modes):
        real, imag = (sum(fields[p * modes + m][part] for p in range(positions)) for part in range(2))
        keep_ref[m] = jnp.where(core == 0, real, imag)
        send_ref[m] = jnp.where(core == 0, imag, real)


def lay(frame_ref, layer, part, offset_ref, block, first):
    extent = block.shape[-1]
    row, col = offset_ref[0], offset_ref[1]
    rows = pl.ds(pl.multiple_of(row // ROWS * ROWS, ROWS), extent + ROWS)
    cols = pl.ds(pl.multiple_of(col // extent * extent, extent), 2 * extent)
    block = jnp.concatenate([block, jnp.zeros((ROWS, extent), F32)], 0)
    block = pltpu.roll(block, lax.rem(row, ROWS), 0)
    wide = pltpu.roll(jnp.concatenate([block, jnp.zeros_like(block)], 1), lax.rem(col, extent), 1)
    frame_ref[layer, part, rows, cols] = wide if first else wide + frame_ref[layer, part, rows, cols]


VMEM = pl.BlockSpec(memory_space=pltpu.VMEM)
SMEM = pl.BlockSpec(memory_space=pltpu.SMEM)


def kernel_call(kernel, name, scalars, arrays, outs, scratch=(), flops=0):
    sizes = sum(math.prod(a.shape) * a.dtype.itemsize for a in arrays)
    return pl.pallas_call(
        kernel,
        out_shape=[jax.ShapeDtypeStruct(shape, dtype) for shape, dtype in outs],
        in_specs=[SMEM] * len(scalars) + [VMEM] * len(arrays),
        out_specs=[SMEM if dtype == jnp.int32 else VMEM for _, dtype in outs],
        scratch_shapes=[pltpu.VMEM(shape, F32) for shape in scratch],
        compiler_params=pltpu.CompilerParams(vmem_limit_bytes=24 << 20),
        cost_estimate=pl.CostEstimate(flops=flops, bytes_accessed=sizes, transcendentals=0),
        name=name,
    )(*scalars, *arrays)


def local(object_slices, probe, prop_phase, scan_offsets, measured):
    own_tile = object_slices[0]
    layers = own_tile.shape[0]
    tile_side = own_tile.shape[-1]
    extent = probe.shape[-1]
    tiles = lax.axis_size("tile")
    shares = lax.axis_size("batch")
    tall = tiles > TGX
    share = lax.axis_index("batch").reshape(1)
    core = share & 1
    half = tile_side // 2
    offset = scan_offsets[0, 0]
    table = fourier_tables(extent)

    field = (extent, extent)
    paired = not tall and shares == 4
    offsets, targets = [offset], [measured[0, 0]]
    own, prop, probe_in, table_in = kernel_call(
        own_kernel, "own_windows", offsets, [own_tile, prop_phase, probe, table],
        [((layers, 2) + field, F32), ((2,) + field, F32), (probe.shape, F32), (table.shape, BF16)],
    )
    owns = [own]
    if paired:
        offsets.append(after(exchanged(offset, "batch", 2), own))
        (partner_own,) = kernel_call(
            partner_kernel, "partner_windows", [offsets[1]], [own_tile], [((layers, 2) + field, F32)]
        )
        owns.append(partner_own)
        targets.append(exchanged(measured[0, 0], "batch", 2))
    positions = len(offsets)
    strip = lax.dynamic_slice(own_tile, (0, 0, core[0] * half, 0), (layers, 2, half, extent))
    strip = after(passed_along(strip, "tile", -1), *owns, *targets)
    pieces = [strip, exchanged(strip, "batch", 1)]
    if tall:
        rim = own_tile[:, :, :extent]
        pieces.append(passed_along(rim, "tile", -TGX))
        pieces.append(passed_along(rim[..., :extent], "tile", -TGX - 1))
    cols = tile_side + extent
    frame_rows = tile_side + (extent if tall else 0)
    share_rows = tile_side // shares if paired else frame_rows
    kept, given, probe_keep, probe_send = kernel_call(
        functools.partial(wave_kernel, positions), "wave_gradients", offsets + [jnp.concatenate([core, share])],
        owns + [probe_in, prop, table_in] + targets + pieces,
        [((layers, 2, share_rows, cols), F32)] * 2 + [(probe.shape[:1] + field, F32)] * 2,
        [(layers, 2, tile_side, extent), (layers, 2, frame_rows + ROWS, cols)],
    )

    got = exchanged(probe_send, "batch", 1)
    rounds = [] if paired else [("batch", 1 << k) for k in range(1, (shares - 1).bit_length())]
    rounds += [("tile", 1 << k) for k in range((tiles - 1).bit_length())]
    if paired:
        total = probe_keep + got
        summed = kept + exchanged(given, "batch", 1)
        landed = passed_along(summed[:, :, :, tile_side:], "tile", 1)
        object_share = summed[:, :, :, :tile_side].at[:, :, :, :extent].add(landed)
        beside = [(summed,)]
    else:
        total = probe_keep + got
        core_grad = kept[:, :, :tile_side, :tile_side]
        parts = [(1, kept[:, :, :tile_side, tile_side:])]
        if tall:
            parts.append((TGX, kept[:, :, tile_side:, :tile_side]))
            parts.append((TGX + 1, kept[:, :, tile_side:, tile_side:]))
        for distance, part in parts:
            landed = passed_along(part, "tile", distance)
            core_grad = core_grad.at[:, :, : landed.shape[2], : landed.shape[3]].add(landed)
        object_share = lax.psum_scatter(core_grad, "batch", scatter_dimension=2, tiled=True)
        beside = []
    if paired:
        nodes = range(tiles * shares)
        for k in range(len(rounds)):
            even, odd = shares * rounds[k][1], shares * rounds[(0, 2, 1)[k]][1]
            got = lax.ppermute(total, ("tile", "batch"), [(i, i ^ (odd if i % 2 else even)) for i in nodes])
            total = total + (after(got, *beside[k]) if k < len(beside) else got)
    else:
        for axis, bit in rounds:
            total = total + exchanged(total, axis, bit)
    total = total / (tiles * shares)
    other = exchanged(total, "batch", 1)
    even = core[0] == 0
    probe_step = jnp.stack([jnp.where(even, total, other), jnp.where(even, other, total)], 1)
    return (object_share[None], probe_step)


def solution(mesh):
    in_specs = (
        P("tile", None, None, None, None),
        P(),
        P(),
        P("tile", "batch", None),
        P("tile", "batch", None, None),
    )
    out_specs = (P("tile", None, None, "batch", None), P())
    return jax.shard_map(local, mesh=mesh, in_specs=in_specs, out_specs=out_specs, check_vma=False)
```

```python
import functools
import math

import jax
import jax.numpy as jnp
import numpy as np
from jax import lax
from jax.experimental import pallas as pl
from jax.experimental.pallas import tpu as pltpu
from jax.sharding import PartitionSpec as P

TGX = 8


LOSS_SCALE = 0.05

F32 = jnp.float32
BF16 = jnp.bfloat16
ROWS = 8


def passed_along(block, axis, distance):
    devices = range(lax.axis_size(axis))
    route = [(i - distance, i) for i in devices if i - distance in devices]
    return lax.ppermute(block, axis, route)


def exchanged(block, axis, bit):
    return lax.ppermute(block, axis, [(i, i ^ bit) for i in range(lax.axis_size(axis))])


def after(value, *others):
    return lax.optimization_barrier((value, *others))[0]


def fourier_tables(extent):
    indices = np.arange(extent)
    phases = (indices[:, None] * indices[None, :] % extent) * (2.0 * math.pi / extent)
    tables = np.stack([np.cos(phases), -np.sin(phases)]).astype(np.float32) / np.float32(math.sqrt(extent))
    high = tables.astype(BF16)
    low = (tables - high.astype(np.float32)).astype(BF16)
    return jnp.asarray(np.stack([high, low]))


def split(value):
    high = value.astype(BF16)
    return high, (value - high.astype(F32)).astype(BF16)


def product(left_op, right_op):
    dot = functools.partial(jnp.dot, preferred_element_type=F32)
    return dot(left_op[0], right_op[0]) + (dot(left_op[0], right_op[1]) + dot(left_op[1], right_op[0]))


def block_matrix(cos_part, sin_part):
    return jnp.concatenate(
        [jnp.concatenate([cos_part, sin_part], 1), jnp.concatenate([-sin_part, cos_part], 1)], 0
    )


def transform(fields, on_left, on_right):
    outs = []
    for k in range(0, len(fields), 2):
        outs += transform_pair(fields[k : k + 2], on_left, on_right)
    return outs


def transform_pair(fields, on_left, on_right):
    extent = fields[0][0].shape[0]
    stacked = jnp.concatenate(
        [jnp.concatenate([f[part] for f in fields], 1) for part in range(2)], 0
    )
    left = product(on_left, split(stacked))
    stacked = jnp.concatenate(
        [
            jnp.concatenate(
                [left[part * extent : (part + 1) * extent, m * extent : (m + 1) * extent] for part in range(2)], 1
            )
            for m in range(len(fields))
        ],
        0,
    )
    out = product(split(stacked), on_right)
    return [
        tuple(
            out[m * extent : (m + 1) * extent, part * extent : (part + 1) * extent] for part in range(2)
        )
        for m in range(len(fields))
    ]


def times(a, b):
    return (a[0] * b[0] - a[1] * b[1], a[0] * b[1] + a[1] * b[0])


def times_conj(a, b):
    return (a[0] * b[0] + a[1] * b[1], a[1] * b[0] - a[0] * b[1])


def rows_from(row, extent, tile_side):
    span = extent + ROWS
    first = jnp.minimum(row // ROWS * ROWS, tile_side - span)
    return pl.ds(pl.multiple_of(first, ROWS), span), row - first


def cut(wide, row, col, extent):
    rows, cols = wide.shape
    wide = pltpu.roll(wide, lax.rem(cols - col, cols), 1)[:, :extent]
    return pltpu.roll(wide, lax.rem(rows - row, rows), 0)[:extent]


def own_windows(row, col, tile_ref, own_ref):
    extent = own_ref.shape[-1]
    rows, shift = rows_from(row, extent, tile_ref.shape[-1])
    for layer in range(tile_ref.shape[0]):
        for part in range(2):
            own_ref[layer, part] = cut(tile_ref[layer, part, rows, :], shift, col, extent)


def own_kernel(offset_ref, tile_ref, phase_ref, probe_in_ref, table_in_ref, own_ref, prop_ref, probe_ref, table_ref):
    own_windows(offset_ref[0], offset_ref[1], tile_ref, own_ref)
    prop_ref[0] = jnp.cos(phase_ref[...])
    prop_ref[1] = jnp.sin(phase_ref[...])
    probe_ref[...] = probe_in_ref[...]
    table_ref[...] = table_in_ref[...]


def partner_kernel(offset_ref, tile_ref, own_ref):
    own_windows(offset_ref[0], offset_ref[1], tile_ref, own_ref)


def whole_windows(offset_refs, core_ref, own_refs, pieces, strip_ref):
    mine_ref, other_ref = pieces[:2]
    layers, _, half, extent = mine_ref.shape
    tile_side = 2 * half
    core = core_ref[0]
    strip_ref[:, :, pl.ds(pl.multiple_of(core * half, half), half), :] = mine_ref[...]
    strip_ref[:, :, pl.ds(pl.multiple_of((1 - core) * half, half), half), :] = other_ref[...]

    def block(layer, part, p):
        row, col = offset_refs[p][0], offset_refs[p][1]
        rows, shift = rows_from(row, extent, tile_side)
        past_row = lax.broadcasted_iota(jnp.int32, (extent, extent), 0) >= tile_side - row
        past_col = lax.broadcasted_iota(jnp.int32, (extent, extent), 1) >= tile_side - col
        col_in = lax.rem(col, extent)
        row_in = lax.rem(row, extent)
        right = cut(strip_ref[layer, part, rows, :], shift, col_in, extent)
        value = jnp.where(past_col, right, own_refs[p][layer, part])
        if len(pieces) > 2:
            below = cut(pieces[2][layer, part], row_in, col, extent)
            corner = cut(pieces[3][layer, part], row_in, col_in, extent)
            value = jnp.where(past_row, jnp.where(past_col, corner, below), value)
        return value

    positions = range(len(offset_refs))
    return [[tuple(block(layer, part, p) for part in range(2)) for p in positions] for layer in range(layers)]


def wave_tools(probe_ref, prop_ref, table_ref):
    probe = [tuple(probe_ref[m, part] for part in range(2)) for m in range(probe_ref.shape[0])]
    prop = (prop_ref[0], prop_ref[1])
    forward = tuple(block_matrix(table_ref[k, 0], table_ref[k, 1]) for k in range(2))
    backward = tuple(block_matrix(table_ref[k, 0], -table_ref[k, 1]) for k in range(2))
    return probe, prop, forward, backward


def propagated(fields, prop, forward, backward):
    fields = transform(fields, backward, forward)
    fields = [times(f, prop) for f in fields]
    return transform(fields, forward, backward)


def wave_kernel(positions, *refs):
    offset_refs, core_ref = refs[:positions], refs[positions]
    own_refs, refs = refs[positions + 1 : 2 * positions + 1], refs[2 * positions + 1 :]
    probe_ref, prop_ref, table_ref = refs[:3]
    measured_refs, pieces = refs[3 : 3 + positions], refs[3 + positions : -6]
    kept_ref, given_ref, keep_ref, send_ref, strip_ref, frame_ref = refs[-6:]
    frame_ref[...] = jnp.zeros_like(frame_ref)
    layers = own_refs[0].shape[0]
    probe, prop, forward, backward = wave_tools(probe_ref, prop_ref, table_ref)
    modes = len(probe)
    windows = whole_windows(offset_refs, core_ref, own_refs, pieces, strip_ref)
    windows = [[w for w in layer for _ in range(modes)] for layer in windows]
    fields = probe * positions
    entering = []
    for layer in range(layers):
        if layer > 0:
            fields = propagated(fields, prop, forward, backward)
        entering.append(fields)
        fields = [times(f, w) for f, w in zip(fields, windows[layer])]
    fields = transform(fields, backward, forward)
    slopes = []
    for p in range(positions):
        intensity = sum(f[0] * f[0] + f[1] * f[1] for f in fields[p * modes : (p + 1) * modes])
        slopes += [(4.0 * LOSS_SCALE) * (intensity - measured_refs[p][...])] * modes
    fields = [(slope * f[0], slope * f[1]) for slope, f in zip(slopes, fields)]
    fields = transform(fields, forward, backward)
    for layer in reversed(range(layers)):
        parts = [times_conj(f, e) for f, e in zip(fields, entering[layer])]
        for p in range(positions):
            for part in range(2):
                block = sum(c[part] for c in parts[p * modes : (p + 1) * modes])
                lay(frame_ref, layer, part, offset_refs[p], block, p == 0)
        fields = [times_conj(f, w) for f, w in zip(fields, windows[layer])]
        if layer > 0:
            fields = transform(fields, backward, forward)
            fields = [times_conj(f, prop) for f in fields]
            fields = transform(fields, forward, backward)
    core = core_ref[0]
    count = kept_ref.shape[2]
    for share, out_ref in ((core_ref[1], kept_ref), (core_ref[1] ^ 1, given_ref)):
        share = share if positions > 1 else 0
        out_ref[...] = frame_ref[:, :, pl.ds(pl.multiple_of(share * count, count), count), :]
    for m in range(modes):
        real, imag = (sum(fields[p * modes + m][part] for p in range(positions)) for part in range(2))
        keep_ref[m] = jnp.where(core == 0, real, imag)
        send_ref[m] = jnp.where(core == 0, imag, real)


def lay(frame_ref, layer, part, offset_ref, block, first):
    extent = block.shape[-1]
    row, col = offset_ref[0], offset_ref[1]
    rows = pl.ds(pl.multiple_of(row // ROWS * ROWS, ROWS), extent + ROWS)
    cols = pl.ds(pl.multiple_of(col // extent * extent, extent), 2 * extent)
    block = jnp.concatenate([block, jnp.zeros((ROWS, extent), F32)], 0)
    block = pltpu.roll(block, lax.rem(row, ROWS), 0)
    wide = pltpu.roll(jnp.concatenate([block, jnp.zeros_like(block)], 1), lax.rem(col, extent), 1)
    frame_ref[layer, part, rows, cols] = wide if first else wide + frame_ref[layer, part, rows, cols]


VMEM = pl.BlockSpec(memory_space=pltpu.VMEM)
SMEM = pl.BlockSpec(memory_space=pltpu.SMEM)


def kernel_call(kernel, name, scalars, arrays, outs, scratch=(), flops=0):
    sizes = sum(math.prod(a.shape) * a.dtype.itemsize for a in arrays)
    return pl.pallas_call(
        kernel,
        out_shape=[jax.ShapeDtypeStruct(shape, dtype) for shape, dtype in outs],
        in_specs=[SMEM] * len(scalars) + [VMEM] * len(arrays),
        out_specs=[SMEM if dtype == jnp.int32 else VMEM for _, dtype in outs],
        scratch_shapes=[pltpu.VMEM(shape, F32) for shape in scratch],
        compiler_params=pltpu.CompilerParams(vmem_limit_bytes=24 << 20),
        cost_estimate=pl.CostEstimate(flops=flops, bytes_accessed=sizes, transcendentals=0),
        name=name,
    )(*scalars, *arrays)


def local(object_slices, probe, prop_phase, scan_offsets, measured):
    own_tile = object_slices[0]
    layers = own_tile.shape[0]
    tile_side = own_tile.shape[-1]
    extent = probe.shape[-1]
    tiles = lax.axis_size("tile")
    shares = lax.axis_size("batch")
    tall = tiles > TGX
    share = lax.axis_index("batch").reshape(1)
    core = share & 1
    half = tile_side // 2
    offset = scan_offsets[0, 0]
    table = fourier_tables(extent)

    field = (extent, extent)
    paired = not tall and shares == 4
    offsets, targets = [offset], [measured[0, 0]]
    own, prop, probe_in, table_in = kernel_call(
        own_kernel, "own_windows", offsets, [own_tile, prop_phase, probe, table],
        [((layers, 2) + field, F32), ((2,) + field, F32), (probe.shape, F32), (table.shape, BF16)],
    )
    owns = [own]
    if paired:
        offsets.append(after(exchanged(offset, "batch", 2), own))
        (partner_own,) = kernel_call(
            partner_kernel, "partner_windows", [offsets[1]], [own_tile], [((layers, 2) + field, F32)]
        )
        owns.append(partner_own)
        targets.append(exchanged(measured[0, 0], "batch", 2))
    positions = len(offsets)
    strip = lax.dynamic_slice(own_tile, (0, 0, core[0] * half, 0), (layers, 2, half, extent))
    strip = after(passed_along(strip, "tile", -1), *owns, *targets)
    pieces = [strip, exchanged(strip, "batch", 1)]
    if tall:
        rim = own_tile[:, :, :extent]
        pieces.append(passed_along(rim, "tile", -TGX))
        pieces.append(passed_along(rim[..., :extent], "tile", -TGX - 1))
    cols = tile_side + extent
    frame_rows = tile_side + (extent if tall else 0)
    share_rows = tile_side // shares if paired else frame_rows
    kept, given, probe_keep, probe_send = kernel_call(
        functools.partial(wave_kernel, positions), "wave_gradients", offsets + [jnp.concatenate([core, share])],
        owns + [probe_in, prop, table_in] + targets + pieces,
        [((layers, 2, share_rows, cols), F32)] * 2 + [(probe.shape[:1] + field, F32)] * 2,
        [(layers, 2, tile_side, extent), (layers, 2, frame_rows + ROWS, cols)],
    )

    got = exchanged(probe_send, "batch", 1)
    rounds = [] if paired else [("batch", 1 << k) for k in range(1, (shares - 1).bit_length())]
    rounds += [("tile", 1 << k) for k in range((tiles - 1).bit_length())]
    if paired:
        total = probe_keep + got
        summed = kept + exchanged(after(given, total), "batch", 1)
        landed = passed_along(summed[:, :, :, tile_side:], "tile", 1)
        object_share = summed[:, :, :, :tile_side].at[:, :, :, :extent].add(landed)
        beside = [(summed,)]
    else:
        total = probe_keep + got
        core_grad = kept[:, :, :tile_side, :tile_side]
        parts = [(1, kept[:, :, :tile_side, tile_side:])]
        if tall:
            parts.append((TGX, kept[:, :, tile_side:, :tile_side]))
            parts.append((TGX + 1, kept[:, :, tile_side:, tile_side:]))
        for distance, part in parts:
            landed = passed_along(part, "tile", distance)
            core_grad = core_grad.at[:, :, : landed.shape[2], : landed.shape[3]].add(landed)
        object_share = lax.psum_scatter(core_grad, "batch", scatter_dimension=2, tiled=True)
        beside = []
    if paired:
        nodes = range(tiles * shares)
        for k in range(len(rounds)):
            even, odd = shares * rounds[k][1], shares * rounds[(0, 2, 1)[k]][1]
            got = lax.ppermute(total, ("tile", "batch"), [(i, i ^ (odd if i % 2 else even)) for i in nodes])
            total = total + (after(got, *beside[k]) if k < len(beside) else got)
    else:
        for axis, bit in rounds:
            total = total + exchanged(total, axis, bit)
    total = total / (tiles * shares)
    other = exchanged(total, "batch", 1)
    even = core[0] == 0
    probe_step = jnp.stack([jnp.where(even, total, other), jnp.where(even, other, total)], 1)
    return (object_share[None], probe_step)


def solution(mesh):
    in_specs = (
        P("tile", None, None, None, None),
        P(),
        P(),
        P("tile", "batch", None),
        P("tile", "batch", None, None),
    )
    out_specs = (P("tile", None, None, "batch", None), P())
    return jax.shard_map(local, mesh=mesh, in_specs=in_specs, out_specs=out_specs, check_vma=False)
```

```python
import functools
import math

import jax
import jax.numpy as jnp
import numpy as np
from jax import lax
from jax.experimental import pallas as pl
from jax.experimental.pallas import tpu as pltpu
from jax.sharding import PartitionSpec as P

TGX = 8


LOSS_SCALE = 0.05

F32 = jnp.float32
BF16 = jnp.bfloat16
ROWS = 8


def passed_along(block, axis, distance):
    devices = range(lax.axis_size(axis))
    route = [(i - distance, i) for i in devices if i - distance in devices]
    return lax.ppermute(block, axis, route)


def exchanged(block, axis, bit):
    return lax.ppermute(block, axis, [(i, i ^ bit) for i in range(lax.axis_size(axis))])


def after(value, *others):
    return lax.optimization_barrier((value, *others))[0]


def fourier_tables(extent):
    indices = np.arange(extent)
    phases = (indices[:, None] * indices[None, :] % extent) * (2.0 * math.pi / extent)
    tables = np.stack([np.cos(phases), -np.sin(phases)]).astype(np.float32) / np.float32(math.sqrt(extent))
    high = tables.astype(BF16)
    low = (tables - high.astype(np.float32)).astype(BF16)
    return jnp.asarray(np.stack([high, low]))


def split(value):
    high = value.astype(BF16)
    return high, (value - high.astype(F32)).astype(BF16)


def product(left_op, right_op):
    dot = functools.partial(jnp.dot, preferred_element_type=F32)
    return dot(left_op[0], right_op[0]) + (dot(left_op[0], right_op[1]) + dot(left_op[1], right_op[0]))


def block_matrix(cos_part, sin_part):
    return jnp.concatenate(
        [jnp.concatenate([cos_part, sin_part], 1), jnp.concatenate([-sin_part, cos_part], 1)], 0
    )


def transform(fields, on_left, on_right):
    extent = fields[0][0].shape[0]
    lefts = []
    for k in range(0, len(fields), 2):
        stacked = [jnp.concatenate([f[part] for f in fields[k : k + 2]], 1) for part in range(2)]
        pair = split(jnp.concatenate(stacked, 0))
        upper, lower = (tuple(t[at : at + extent] for t in on_left) for at in (0, extent))
        lefts.append((product(upper, pair), product(lower, pair)))
    outs = []
    for left in lefts:
        for at in range(0, left[0].shape[1], extent):
            row = jnp.concatenate([half[:, at : at + extent] for half in left], 1)
            out = product(split(row), on_right)
            outs.append((out[:, :extent], out[:, extent:]))
    return outs


def times(a, b):
    return (a[0] * b[0] - a[1] * b[1], a[0] * b[1] + a[1] * b[0])


def times_conj(a, b):
    return (a[0] * b[0] + a[1] * b[1], a[1] * b[0] - a[0] * b[1])


def rows_from(row, extent, tile_side):
    span = extent + ROWS
    first = jnp.minimum(row // ROWS * ROWS, tile_side - span)
    return pl.ds(pl.multiple_of(first, ROWS), span), row - first


def cut(wide, row, col, extent):
    rows, cols = wide.shape
    wide = pltpu.roll(wide, lax.rem(cols - col, cols), 1)[:, :extent]
    return pltpu.roll(wide, lax.rem(rows - row, rows), 0)[:extent]


def own_windows(row, col, tile_ref, own_ref):
    extent = own_ref.shape[-1]
    rows, shift = rows_from(row, extent, tile_ref.shape[-1])
    for layer in range(tile_ref.shape[0]):
        for part in range(2):
            own_ref[layer, part] = cut(tile_ref[layer, part, rows, :], shift, col, extent)


def own_kernel(offset_ref, tile_ref, phase_ref, probe_in_ref, table_in_ref, own_ref, prop_ref, probe_ref, table_ref):
    own_windows(offset_ref[0], offset_ref[1], tile_ref, own_ref)
    prop_ref[0] = jnp.cos(phase_ref[...])
    prop_ref[1] = jnp.sin(phase_ref[...])
    probe_ref[...] = probe_in_ref[...]
    table_ref[...] = table_in_ref[...]


def partner_kernel(offset_ref, tile_ref, own_ref):
    own_windows(offset_ref[0], offset_ref[1], tile_ref, own_ref)


def whole_windows(offset_refs, core_ref, own_refs, pieces, strip_ref):
    mine_ref, other_ref = pieces[:2]
    layers, _, half, extent = mine_ref.shape
    tile_side = 2 * half
    core = core_ref[0]
    strip_ref[:, :, pl.ds(pl.multiple_of(core * half, half), half), :] = mine_ref[...]
    strip_ref[:, :, pl.ds(pl.multiple_of((1 - core) * half, half), half), :] = other_ref[...]

    def block(layer, part, p):
        row, col = offset_refs[p][0], offset_refs[p][1]
        rows, shift = rows_from(row, extent, tile_side)
        past_row = lax.broadcasted_iota(jnp.int32, (extent, extent), 0) >= tile_side - row
        past_col = lax.broadcasted_iota(jnp.int32, (extent, extent), 1) >= tile_side - col
        col_in = lax.rem(col, extent)
        row_in = lax.rem(row, extent)
        right = cut(strip_ref[layer, part, rows, :], shift, col_in, extent)
        value = jnp.where(past_col, right, own_refs[p][layer, part])
        if len(pieces) > 2:
            below = cut(pieces[2][layer, part], row_in, col, extent)
            corner = cut(pieces[3][layer, part], row_in, col_in, extent)
            value = jnp.where(past_row, jnp.where(past_col, corner, below), value)
        return value

    positions = range(len(offset_refs))
    return [[tuple(block(layer, part, p) for part in range(2)) for p in positions] for layer in range(layers)]


def wave_tools(probe_ref, prop_ref, table_ref):
    probe = [tuple(probe_ref[m, part] for part in range(2)) for m in range(probe_ref.shape[0])]
    prop = (prop_ref[0], prop_ref[1])
    forward = tuple(block_matrix(table_ref[k, 0], table_ref[k, 1]) for k in range(2))
    backward = tuple(block_matrix(table_ref[k, 0], -table_ref[k, 1]) for k in range(2))
    return probe, prop, forward, backward


def propagated(fields, prop, forward, backward):
    fields = transform(fields, backward, forward)
    fields = [times(f, prop) for f in fields]
    return transform(fields, forward, backward)


def wave_kernel(positions, *refs):
    offset_refs, core_ref = refs[:positions], refs[positions]
    own_refs, refs = refs[positions + 1 : 2 * positions + 1], refs[2 * positions + 1 :]
    probe_ref, prop_ref, table_ref = refs[:3]
    measured_refs, pieces = refs[3 : 3 + positions], refs[3 + positions : -6]
    kept_ref, given_ref, keep_ref, send_ref, strip_ref, frame_ref = refs[-6:]
    frame_ref[...] = jnp.zeros_like(frame_ref)
    layers = own_refs[0].shape[0]
    probe, prop, forward, backward = wave_tools(probe_ref, prop_ref, table_ref)
    modes = len(probe)
    windows = whole_windows(offset_refs, core_ref, own_refs, pieces, strip_ref)
    windows = [[w for w in layer for _ in range(modes)] for layer in windows]
    fields = probe * positions
    entering = []
    for layer in range(layers):
        if layer > 0:
            fields = propagated(fields, prop, forward, backward)
        entering.append(fields)
        fields = [times(f, w) for f, w in zip(fields, windows[layer])]
    fields = transform(fields, backward, forward)
    slopes = []
    for p in range(positions):
        intensity = sum(f[0] * f[0] + f[1] * f[1] for f in fields[p * modes : (p + 1) * modes])
        slopes += [(4.0 * LOSS_SCALE) * (intensity - measured_refs[p][...])] * modes
    fields = [(slope * f[0], slope * f[1]) for slope, f in zip(slopes, fields)]
    fields = transform(fields, forward, backward)
    for layer in reversed(range(layers)):
        parts = [times_conj(f, e) for f, e in zip(fields, entering[layer])]
        for p in range(positions):
            for part in range(2):
                block = sum(c[part] for c in parts[p * modes : (p + 1) * modes])
                lay(frame_ref, layer, part, offset_refs[p], block, p == 0)
        fields = [times_conj(f, w) for f, w in zip(fields, windows[layer])]
        if layer > 0:
            fields = transform(fields, backward, forward)
            fields = [times_conj(f, prop) for f in fields]
            fields = transform(fields, forward, backward)
    core = core_ref[0]
    count = kept_ref.shape[2]
    for share, out_ref in ((core_ref[1], kept_ref), (core_ref[1] ^ 1, given_ref)):
        share = share if positions > 1 else 0
        out_ref[...] = frame_ref[:, :, pl.ds(pl.multiple_of(share * count, count), count), :]
    for m in range(modes):
        real, imag = (sum(fields[p * modes + m][part] for p in range(positions)) for part in range(2))
        keep_ref[m] = jnp.where(core == 0, real, imag)
        send_ref[m] = jnp.where(core == 0, imag, real)


def lay(frame_ref, layer, part, offset_ref, block, first):
    extent = block.shape[-1]
    row, col = offset_ref[0], offset_ref[1]
    rows = pl.ds(pl.multiple_of(row // ROWS * ROWS, ROWS), extent + ROWS)
    cols = pl.ds(pl.multiple_of(col // extent * extent, extent), 2 * extent)
    block = jnp.concatenate([block, jnp.zeros((ROWS, extent), F32)], 0)
    block = pltpu.roll(block, lax.rem(row, ROWS), 0)
    wide = pltpu.roll(jnp.concatenate([block, jnp.zeros_like(block)], 1), lax.rem(col, extent), 1)
    frame_ref[layer, part, rows, cols] = wide if first else wide + frame_ref[layer, part, rows, cols]


VMEM = pl.BlockSpec(memory_space=pltpu.VMEM)
SMEM = pl.BlockSpec(memory_space=pltpu.SMEM)


def kernel_call(kernel, name, scalars, arrays, outs, scratch=(), flops=0):
    sizes = sum(math.prod(a.shape) * a.dtype.itemsize for a in arrays)
    return pl.pallas_call(
        kernel,
        out_shape=[jax.ShapeDtypeStruct(shape, dtype) for shape, dtype in outs],
        in_specs=[SMEM] * len(scalars) + [VMEM] * len(arrays),
        out_specs=[SMEM if dtype == jnp.int32 else VMEM for _, dtype in outs],
        scratch_shapes=[pltpu.VMEM(shape, F32) for shape in scratch],
        compiler_params=pltpu.CompilerParams(vmem_limit_bytes=24 << 20),
        cost_estimate=pl.CostEstimate(flops=flops, bytes_accessed=sizes, transcendentals=0),
        name=name,
    )(*scalars, *arrays)


def local(object_slices, probe, prop_phase, scan_offsets, measured):
    own_tile = object_slices[0]
    layers = own_tile.shape[0]
    tile_side = own_tile.shape[-1]
    extent = probe.shape[-1]
    tiles = lax.axis_size("tile")
    shares = lax.axis_size("batch")
    tall = tiles > TGX
    share = lax.axis_index("batch").reshape(1)
    core = share & 1
    half = tile_side // 2
    offset = scan_offsets[0, 0]
    table = fourier_tables(extent)

    field = (extent, extent)
    paired = not tall and shares == 4
    offsets, targets = [offset], [measured[0, 0]]
    own, prop, probe_in, table_in = kernel_call(
        own_kernel, "own_windows", offsets, [own_tile, prop_phase, probe, table],
        [((layers, 2) + field, F32), ((2,) + field, F32), (probe.shape, F32), (table.shape, BF16)],
    )
    owns = [own]
    if paired:
        offsets.append(after(exchanged(offset, "batch", 2), own))
        (partner_own,) = kernel_call(
            partner_kernel, "partner_windows", [offsets[1]], [own_tile], [((layers, 2) + field, F32)]
        )
        owns.append(partner_own)
        targets.append(exchanged(measured[0, 0], "batch", 2))
    positions = len(offsets)
    strip = lax.dynamic_slice(own_tile, (0, 0, core[0] * half, 0), (layers, 2, half, extent))
    strip = after(passed_along(strip, "tile", -1), *owns, *targets)
    pieces = [strip, exchanged(strip, "batch", 1)]
    if tall:
        rim = own_tile[:, :, :extent]
        pieces.append(passed_along(rim, "tile", -TGX))
        pieces.append(passed_along(rim[..., :extent], "tile", -TGX - 1))
    cols = tile_side + extent
    frame_rows = tile_side + (extent if tall else 0)
    share_rows = tile_side // shares if paired else frame_rows
    kept, given, probe_keep, probe_send = kernel_call(
        functools.partial(wave_kernel, positions), "wave_gradients", offsets + [jnp.concatenate([core, share])],
        owns + [probe_in, prop, table_in] + targets + pieces,
        [((layers, 2, share_rows, cols), F32)] * 2 + [(probe.shape[:1] + field, F32)] * 2,
        [(layers, 2, tile_side, extent), (layers, 2, frame_rows + ROWS, cols)],
    )

    got = exchanged(probe_send, "batch", 1)
    rounds = [] if paired else [("batch", 1 << k) for k in range(1, (shares - 1).bit_length())]
    rounds += [("tile", 1 << k) for k in range((tiles - 1).bit_length())]
    if paired:
        total = probe_keep + got
        summed = kept + exchanged(after(given, total), "batch", 1)
        landed = passed_along(summed[:, :, :, tile_side:], "tile", 1)
        object_share = summed[:, :, :, :tile_side].at[:, :, :, :extent].add(landed)
        beside = [(summed,)]
    else:
        total = probe_keep + got
        core_grad = kept[:, :, :tile_side, :tile_side]
        parts = [(1, kept[:, :, :tile_side, tile_side:])]
        if tall:
            parts.append((TGX, kept[:, :, tile_side:, :tile_side]))
            parts.append((TGX + 1, kept[:, :, tile_side:, tile_side:]))
        for distance, part in parts:
            landed = passed_along(part, "tile", distance)
            core_grad = core_grad.at[:, :, : landed.shape[2], : landed.shape[3]].add(landed)
        object_share = lax.psum_scatter(core_grad, "batch", scatter_dimension=2, tiled=True)
        beside = []
    if paired:
        nodes = range(tiles * shares)
        orders = [rounds, rounds[:1] + rounds[:0:-1]]
        for k in range(len(rounds)):
            bits = [shares * order[k][1] for order in orders]
            got = lax.ppermute(total, ("tile", "batch"), [(i, i ^ bits[i % 2]) for i in nodes])
            total = total + (after(got, *beside[k]) if k < len(beside) else got)
    else:
        for axis, bit in rounds:
            total = total + exchanged(total, axis, bit)
    total = total / (tiles * shares)
    other = exchanged(total, "batch", 1)
    even = core[0] == 0
    probe_step = jnp.stack([jnp.where(even, total, other), jnp.where(even, other, total)], 1)
    return (object_share[None], probe_step)


def solution(mesh):
    in_specs = (
        P("tile", None, None, None, None),
        P(),
        P(),
        P("tile", "batch", None),
        P("tile", "batch", None, None),
    )
    out_specs = (P("tile", None, None, "batch", None), P())
    return jax.shard_map(local, mesh=mesh, in_specs=in_specs, out_specs=out_specs, check_vma=False)
```

```python
import functools
import math

import jax
import jax.numpy as jnp
import numpy as np
from jax import lax
from jax.experimental import pallas as pl
from jax.experimental.pallas import tpu as pltpu
from jax.sharding import PartitionSpec as P

TGX = 8


LOSS_SCALE = 0.05

F32 = jnp.float32
BF16 = jnp.bfloat16
ROWS = 8


def passed_along(block, axis, distance):
    devices = range(lax.axis_size(axis))
    route = [(i - distance, i) for i in devices if i - distance in devices]
    return lax.ppermute(block, axis, route)


def exchanged(block, axis, bit):
    return lax.ppermute(block, axis, [(i, i ^ bit) for i in range(lax.axis_size(axis))])


def after(value, *others):
    return lax.optimization_barrier((value, *others))[0]


def fourier_tables(extent):
    indices = np.arange(extent)
    phases = (indices[:, None] * indices[None, :] % extent) * (2.0 * math.pi / extent)
    tables = np.stack([np.cos(phases), -np.sin(phases)]).astype(np.float32) / np.float32(math.sqrt(extent))
    high = tables.astype(BF16)
    low = (tables - high.astype(np.float32)).astype(BF16)
    return jnp.asarray(np.stack([high, low]))


def split(value):
    high = value.astype(BF16)
    return high, (value - high.astype(F32)).astype(BF16)


def product(left_op, right_op):
    dot = functools.partial(jnp.dot, preferred_element_type=F32)
    return dot(left_op[0], right_op[0]) + (dot(left_op[0], right_op[1]) + dot(left_op[1], right_op[0]))


def block_matrix(cos_part, sin_part):
    return jnp.concatenate(
        [jnp.concatenate([cos_part, sin_part], 1), jnp.concatenate([-sin_part, cos_part], 1)], 0
    )


def transform(fields, on_left, on_right):
    extent = fields[0][0].shape[0]
    lefts = []
    for k in range(0, len(fields), 2):
        stacked = [jnp.concatenate([f[part] for f in fields[k : k + 2]], 1) for part in range(2)]
        pair = split(jnp.concatenate(stacked, 0))
        upper, lower = (tuple(t[at : at + extent] for t in on_left) for at in (0, extent))
        lefts.append((product(upper, pair), product(lower, pair)))
    outs = []
    for left in lefts:
        for at in range(0, left[0].shape[1], extent):
            row = jnp.concatenate([half[:, at : at + extent] for half in left], 1)
            out = product(split(row), on_right)
            outs.append((out[:, :extent], out[:, extent:]))
    return outs


def times(a, b):
    return (a[0] * b[0] - a[1] * b[1], a[0] * b[1] + a[1] * b[0])


def times_conj(a, b):
    return (a[0] * b[0] + a[1] * b[1], a[1] * b[0] - a[0] * b[1])


def rows_from(row, extent, tile_side):
    span = extent + ROWS
    first = jnp.minimum(row // ROWS * ROWS, tile_side - span)
    return pl.ds(pl.multiple_of(first, ROWS), span), row - first


def cut(wide, row, col, extent):
    rows, cols = wide.shape
    wide = pltpu.roll(wide, lax.rem(cols - col, cols), 1)[:, :extent]
    return pltpu.roll(wide, lax.rem(rows - row, rows), 0)[:extent]


def own_windows(row, col, tile_ref, own_ref):
    extent = own_ref.shape[-1]
    rows, shift = rows_from(row, extent, tile_ref.shape[-1])
    for layer in range(tile_ref.shape[0]):
        for part in range(2):
            own_ref[layer, part] = cut(tile_ref[layer, part, rows, :], shift, col, extent)


def own_kernel(offset_ref, tile_ref, phase_ref, probe_in_ref, table_in_ref, own_ref, prop_ref, probe_ref, table_ref):
    own_windows(offset_ref[0], offset_ref[1], tile_ref, own_ref)
    prop_ref[0] = jnp.cos(phase_ref[...])
    prop_ref[1] = jnp.sin(phase_ref[...])
    probe_ref[...] = probe_in_ref[...]
    table_ref[...] = table_in_ref[...]


def partner_kernel(offset_ref, tile_ref, own_ref):
    own_windows(offset_ref[0], offset_ref[1], tile_ref, own_ref)


def whole_windows(offset_refs, core_ref, own_refs, pieces, strip_ref):
    mine_ref, other_ref = pieces[:2]
    layers, _, half, extent = mine_ref.shape
    tile_side = 2 * half
    core = core_ref[0]
    strip_ref[:, :, pl.ds(pl.multiple_of(core * half, half), half), :] = mine_ref[...]
    strip_ref[:, :, pl.ds(pl.multiple_of((1 - core) * half, half), half), :] = other_ref[...]

    def block(layer, part, p):
        row, col = offset_refs[p][0], offset_refs[p][1]
        rows, shift = rows_from(row, extent, tile_side)
        past_row = lax.broadcasted_iota(jnp.int32, (extent, extent), 0) >= tile_side - row
        past_col = lax.broadcasted_iota(jnp.int32, (extent, extent), 1) >= tile_side - col
        col_in = lax.rem(col, extent)
        row_in = lax.rem(row, extent)
        right = cut(strip_ref[layer, part, rows, :], shift, col_in, extent)
        value = jnp.where(past_col, right, own_refs[p][layer, part])
        if len(pieces) > 2:
            below = cut(pieces[2][layer, part], row_in, col, extent)
            corner = cut(pieces[3][layer, part], row_in, col_in, extent)
            value = jnp.where(past_row, jnp.where(past_col, corner, below), value)
        return value

    positions = range(len(offset_refs))
    return [[tuple(block(layer, part, p) for part in range(2)) for p in positions] for layer in range(layers)]


def wave_tools(probe_ref, prop_ref, table_ref):
    probe = [tuple(probe_ref[m, part] for part in range(2)) for m in range(probe_ref.shape[0])]
    prop = (prop_ref[0], prop_ref[1])
    forward = tuple(block_matrix(table_ref[k, 0], table_ref[k, 1]) for k in range(2))
    backward = tuple(block_matrix(table_ref[k, 0], -table_ref[k, 1]) for k in range(2))
    return probe, prop, forward, backward


def propagated(fields, prop, forward, backward):
    fields = transform(fields, backward, forward)
    fields = [times(f, prop) for f in fields]
    return transform(fields, forward, backward)


def wave_kernel(positions, *refs):
    offset_refs, core_ref = refs[:positions], refs[positions]
    own_refs, refs = refs[positions + 1 : 2 * positions + 1], refs[2 * positions + 1 :]
    probe_ref, prop_ref, table_ref = refs[:3]
    measured_refs, pieces = refs[3 : 3 + positions], refs[3 + positions : -6]
    kept_ref, given_ref, keep_ref, send_ref, strip_ref, frame_ref = refs[-6:]
    frame_ref[...] = jnp.zeros_like(frame_ref)
    layers = own_refs[0].shape[0]
    probe, prop, forward, backward = wave_tools(probe_ref, prop_ref, table_ref)
    modes = len(probe)
    windows = whole_windows(offset_refs, core_ref, own_refs, pieces, strip_ref)
    windows = [[w for w in layer for _ in range(modes)] for layer in windows]
    fields = probe * positions
    entering = []
    for layer in range(layers):
        if layer > 0:
            fields = propagated(fields, prop, forward, backward)
        entering.append(fields)
        fields = [times(f, w) for f, w in zip(fields, windows[layer])]
    fields = transform(fields, backward, forward)
    slopes = []
    for p in range(positions):
        intensity = sum(f[0] * f[0] + f[1] * f[1] for f in fields[p * modes : (p + 1) * modes])
        slopes += [(4.0 * LOSS_SCALE) * (intensity - measured_refs[p][...])] * modes
    fields = [(slope * f[0], slope * f[1]) for slope, f in zip(slopes, fields)]
    fields = transform(fields, forward, backward)
    for layer in reversed(range(layers)):
        parts = [times_conj(f, e) for f, e in zip(fields, entering[layer])]
        for p in range(positions):
            for part in range(2):
                block = sum(c[part] for c in parts[p * modes : (p + 1) * modes])
                lay(frame_ref, layer, part, offset_refs[p], block, p == 0)
        fields = [times_conj(f, w) for f, w in zip(fields, windows[layer])]
        if layer > 0:
            fields = transform(fields, backward, forward)
            fields = [times_conj(f, prop) for f in fields]
            fields = transform(fields, forward, backward)
    core = core_ref[0]
    count = kept_ref.shape[2]
    for share, out_ref in ((core_ref[1], kept_ref), (core_ref[1] ^ 1, given_ref)):
        share = share if positions > 1 else 0
        out_ref[...] = frame_ref[:, :, pl.ds(pl.multiple_of(share * count, count), count), :]
    for m in range(modes):
        real, imag = (sum(fields[p * modes + m][part] for p in range(positions)) for part in range(2))
        keep_ref[m] = jnp.where(core == 0, real, imag)
        send_ref[m] = jnp.where(core == 0, imag, real)


def lay(frame_ref, layer, part, offset_ref, block, first):
    extent = block.shape[-1]
    row, col = offset_ref[0], offset_ref[1]
    rows = pl.ds(pl.multiple_of(row // ROWS * ROWS, ROWS), extent + ROWS)
    cols = pl.ds(pl.multiple_of(col // extent * extent, extent), 2 * extent)
    block = jnp.concatenate([block, jnp.zeros((ROWS, extent), F32)], 0)
    block = pltpu.roll(block, lax.rem(row, ROWS), 0)
    wide = pltpu.roll(jnp.concatenate([block, jnp.zeros_like(block)], 1), lax.rem(col, extent), 1)
    frame_ref[layer, part, rows, cols] = wide if first else wide + frame_ref[layer, part, rows, cols]


VMEM = pl.BlockSpec(memory_space=pltpu.VMEM)
SMEM = pl.BlockSpec(memory_space=pltpu.SMEM)


def kernel_call(kernel, name, scalars, arrays, outs, scratch=(), flops=0):
    sizes = sum(math.prod(a.shape) * a.dtype.itemsize for a in arrays)
    return pl.pallas_call(
        kernel,
        out_shape=[jax.ShapeDtypeStruct(shape, dtype) for shape, dtype in outs],
        in_specs=[SMEM] * len(scalars) + [VMEM] * len(arrays),
        out_specs=[SMEM if dtype == jnp.int32 else VMEM for _, dtype in outs],
        scratch_shapes=[pltpu.VMEM(shape, F32) for shape in scratch],
        compiler_params=pltpu.CompilerParams(vmem_limit_bytes=24 << 20),
        cost_estimate=pl.CostEstimate(flops=flops, bytes_accessed=sizes, transcendentals=0),
        name=name,
    )(*scalars, *arrays)


def local(object_slices, probe, prop_phase, scan_offsets, measured):
    own_tile = object_slices[0]
    layers = own_tile.shape[0]
    tile_side = own_tile.shape[-1]
    extent = probe.shape[-1]
    tiles = lax.axis_size("tile")
    shares = lax.axis_size("batch")
    tall = tiles > TGX
    share = lax.axis_index("batch").reshape(1)
    core = share & 1
    half = tile_side // 2
    offset = scan_offsets[0, 0]
    table = fourier_tables(extent)

    field = (extent, extent)
    paired = not tall and shares == 4
    offsets, targets = [offset], [measured[0, 0]]
    own, prop, probe_in, table_in = kernel_call(
        own_kernel, "own_windows", offsets, [own_tile, prop_phase, probe, table],
        [((layers, 2) + field, F32), ((2,) + field, F32), (probe.shape, F32), (table.shape, BF16)],
    )
    owns = [own]
    if paired:
        offsets.append(after(exchanged(offset, "batch", 2), own))
        (partner_own,) = kernel_call(
            partner_kernel, "partner_windows", [offsets[1]], [own_tile], [((layers, 2) + field, F32)]
        )
        owns.append(partner_own)
        targets.append(exchanged(measured[0, 0], "batch", 2))
    positions = len(offsets)
    strip = lax.dynamic_slice(own_tile, (0, 0, core[0] * half, 0), (layers, 2, half, extent))
    strip = after(passed_along(strip, "tile", -1), *owns, *targets)
    pieces = [strip, exchanged(strip, "batch", 1)]
    if tall:
        rim = own_tile[:, :, :extent]
        pieces.append(passed_along(rim, "tile", -TGX))
        pieces.append(passed_along(rim[..., :extent], "tile", -TGX - 1))
    cols = tile_side + extent
    frame_rows = tile_side + (extent if tall else 0)
    share_rows = tile_side // shares if paired else frame_rows
    kept, given, probe_keep, probe_send = kernel_call(
        functools.partial(wave_kernel, positions), "wave_gradients", offsets + [jnp.concatenate([core, share])],
        owns + [probe_in, prop, table_in] + targets + pieces,
        [((layers, 2, share_rows, cols), F32)] * 2 + [(probe.shape[:1] + field, F32)] * 2,
        [(layers, 2, tile_side, extent), (layers, 2, frame_rows + ROWS, cols)],
    )

    got = exchanged(probe_send, "batch", 1)
    rounds = [] if paired else [("batch", 1 << k) for k in range(1, (shares - 1).bit_length())]
    rounds += [("tile", 1 << k) for k in range((tiles - 1).bit_length())]
    if paired:
        total = probe_keep + got
        summed = kept + exchanged(after(given, total), "batch", 1)
        landed = passed_along(summed[:, :, :, tile_side:], "tile", 1)
        object_share = summed[:, :, :, :tile_side].at[:, :, :, :extent].add(landed)
        beside = [(summed,)]
    else:
        total = probe_keep + got
        core_grad = kept[:, :, :tile_side, :tile_side]
        parts = [(1, kept[:, :, :tile_side, tile_side:])]
        if tall:
            parts.append((TGX, kept[:, :, tile_side:, :tile_side]))
            parts.append((TGX + 1, kept[:, :, tile_side:, tile_side:]))
        for distance, part in parts:
            landed = passed_along(part, "tile", distance)
            core_grad = core_grad.at[:, :, : landed.shape[2], : landed.shape[3]].add(landed)
        object_share = lax.psum_scatter(core_grad, "batch", scatter_dimension=2, tiled=True)
        beside = []
    if paired:
        nodes = range(tiles * shares)
        orders = [rounds[-1:] + rounds[:-1], rounds]
        for k in range(len(rounds)):
            bits = [shares * order[k][1] for order in orders]
            got = lax.ppermute(total, ("tile", "batch"), [(i, i ^ bits[i % 2]) for i in nodes])
            total = total + (after(got, *beside[k]) if k < len(beside) else got)
    else:
        for axis, bit in rounds:
            total = total + exchanged(total, axis, bit)
    total = total / (tiles * shares)
    other = exchanged(total, "batch", 1)
    even = core[0] == 0
    probe_step = jnp.stack([jnp.where(even, total, other), jnp.where(even, other, total)], 1)
    return (object_share[None], probe_step)


def solution(mesh):
    in_specs = (
        P("tile", None, None, None, None),
        P(),
        P(),
        P("tile", "batch", None),
        P("tile", "batch", None, None),
    )
    out_specs = (P("tile", None, None, "batch", None), P())
    return jax.shard_map(local, mesh=mesh, in_specs=in_specs, out_specs=out_specs, check_vma=False)
```
